32 devices in a mesh: grp: 4 (over z), blk: 8 (over y, x, core).
Axes of the slice: x: 2, y: 2, z: 4, core: 2. Of those that a mesh axis runs over, the one named last changes fastest.
Arguments:
- integrals: bfloat16 [32, 2048, 2048], P('blk', None, 'grp'), as said below
- tile_mask: int32 [16, 16], replicated, may hold values from 0 to 1, as said below
- tile_owner: int32 [16], replicated, may hold values from 0 to 15, as said below
- occupied_tiles: bfloat16 [16384, 128], P(('grp', 'blk')), may hold values from -0.1875 to 0.1875
- occupied_offsets: int32 [8], replicated, may hold values from 0 to 15, as said below
- virtual_tiles: bfloat16 [16384, 128], P(('grp', 'blk')), may hold values from -0.1875 to 0.1875
- virtual_offsets: int32 [8], replicated, may hold values from 0 to 15, as said below
Outputs:
- polarizability: float32 [32, 32], P('blk')
The draws below stay inside these ranges and needn't reach their ends.
Inputs may be any that keep to these rules, and one draw needn't show every extreme that they name: `integrals`: after column slot s is placed at basis tile tile_owner[s], the tensor is symmetric in its two basis indices. `tile_mask`: symmetric, with ones on the diagonal. `tile_owner`: each tile exactly once. `occupied_offsets`: 8 different tile offsets, among them 0 and 15. `virtual_offsets`: 8 different tile offsets, among them 0 and 15.
All inputs are finite; a program needn't handle non-finite values.
Results may differ from the reference program's by a relative error of at most 0.004.
Values may be sent and summed in bfloat16 or wider, within the bound.
No kernel may reach another device: no remote copies, remote signals or barrier semaphores. Data moves between devices by JAX's collectives and lax.ppermute only.
A program may use at most 256 MiB of HBM per device.

```python
import jax
import jax.numpy as jnp
from jax import lax

TW = 128
NT = 16
K = 8
NAUX = 32
NAO = 2048


def owner_order(key):
    return jax.random.permutation(jax.random.fold_in(key, 11), NT).astype(jnp.int32)


def mask_table(key):
    coins = jax.random.randint(jax.random.fold_in(key, 12), (NT, NT), 0, 5)
    upper = jnp.triu((coins < 3).astype(jnp.int32), 1)
    return upper + upper.T + jnp.eye(NT, dtype=jnp.int32)


def offset_set(key):
    middle = 1 + jax.random.permutation(jax.random.fold_in(key, 1), NT - 2)[:K - 2].astype(jnp.int32)
    ends = jnp.array([0, NT - 1], dtype=jnp.int32)
    values = jnp.concatenate([ends, middle]).astype(jnp.int32)
    order = jax.random.permutation(jax.random.fold_in(key, 2), K).astype(jnp.int32)
    return values[order].astype(jnp.int32)


def draw_tile_owner(key, part):
    return owner_order(key)


def draw_tile_mask(key, part):
    return mask_table(key)


def draw_integrals(key, part):
    order = owner_order(key)
    base_key = jax.random.fold_in(key, 13)

    def one_row(index):
        row_key = jax.random.fold_in(base_key, index)
        raw_values = jax.random.normal(row_key, (NAO, NAO), jnp.float32)
        factor = jnp.float32(1.0)
        symmetric = (raw_values + raw_values.T) * (0.7071 * factor)
        placed = symmetric.reshape(NAO, NT, TW)[:, order, :]
        return placed.reshape(NAO, NAO)
    return lax.map(one_row, jnp.arange(NAUX)).astype(jnp.bfloat16)


def draw_occupied_offsets(key, part):
    return offset_set(jax.random.fold_in(key, 21))


def draw_virtual_offsets(key, part):
    return offset_set(jax.random.fold_in(key, 22))


def levels(stream_key, extent, pieces, smallest, largest):
    level = 1.0
    for axis_at, parts in pieces:
        steps = jax.random.uniform(jax.random.fold_in(jax.random.fold_in(stream_key, 6), axis_at), (parts,), jnp.float32, smallest / len(pieces), largest / len(pieces))
        level = level * jnp.repeat(jnp.exp(steps), extent[axis_at] // parts).reshape((-1,) + (1,) * (len(extent) - 1 - axis_at))
    return level


def bell_draw(rng, shape, width, reach, shards=(), kind=jnp.bfloat16):
    gain = levels(rng, shape, shards, -0.22, 0.18) if shards else 1.0
    values = jax.random.normal(rng, shape, jnp.float32) * width * gain
    return jnp.minimum(jnp.maximum(values, -reach), reach).astype(kind)


def setup_inputs(seed: int = 0) -> dict:
    keys = jax.random.split(jax.random.key(seed), 8)
    return {
        "integrals": draw_integrals(jax.random.fold_in(keys[7], 71), 0),
        "tile_mask": draw_tile_mask(jax.random.fold_in(keys[7], 71), 0),
        "tile_owner": draw_tile_owner(jax.random.fold_in(keys[7], 71), 0),
        "occupied_tiles": bell_draw(keys[3], (NT * K * TW, TW), (K * TW) ** -0.5, 0.1875, ((0, 32),)),
        "occupied_offsets": draw_occupied_offsets(jax.random.fold_in(keys[7], 71), 0),
        "virtual_tiles": bell_draw(keys[5], (NT * K * TW, TW), (K * TW) ** -0.5, 0.1875, ((0, 32),)),
        "virtual_offsets": draw_virtual_offsets(jax.random.fold_in(keys[7], 71), 0),
    }


def column_block(integrals, tile_mask, slot_of, tile_index):
    slot = slot_of[tile_index].astype(jnp.int32)
    block = lax.dynamic_slice_in_dim(integrals, (slot * TW).astype(jnp.int32), TW, 2)
    weights = jnp.repeat(tile_mask[:, tile_index], TW).astype(jnp.float32)
    return block.astype(jnp.float32) * weights[None, :, None]


def rounded(values):
    return lax.optimization_barrier(values.astype(jnp.bfloat16)).astype(jnp.float32)


def reference(integrals, tile_mask, tile_owner, occupied_tiles, occupied_offsets, virtual_tiles, virtual_offsets):
    slot_of = jnp.zeros((NT,), jnp.int32).at[tile_owner].set(jnp.arange(NT, dtype=jnp.int32))
    occupied = occupied_tiles.astype(jnp.float32).reshape(NT, K, TW, TW)
    virtual = virtual_tiles.astype(jnp.float32).reshape(NT, K, TW, TW)
    targets = jnp.arange(NT, dtype=jnp.int32)
    sources = ((targets[:, None] - occupied_offsets[None, :]) % NT).astype(jnp.int32)
    picked = occupied[sources, jnp.arange(K, dtype=jnp.int32)[None, :]]

    def one_tile(tile_index, total):
        block = column_block(integrals, tile_mask, slot_of, tile_index)
        tiled = block.reshape(NAUX, NT, TW, TW)
        occupied_half = jnp.zeros((NAUX, NT, TW, TW), jnp.float32)
        virtual_half = jnp.zeros((NAUX, NAO, TW), jnp.float32)
        virtual_rows = lax.dynamic_index_in_dim(virtual, tile_index, 0, keepdims=False)
        for slot in range(K):
            inputs = jnp.take(tiled, sources[:, slot], axis=1)
            occupied_half = occupied_half + jnp.einsum("kmn,pkml->pknl", picked[:, slot], inputs, precision=lax.Precision.HIGHEST)
            partner = ((tile_index + virtual_offsets[slot]) % NT).astype(jnp.int32)
            other = column_block(integrals, tile_mask, slot_of, partner)
            virtual_half = virtual_half + jnp.einsum("pvm,nm->pvn", other, virtual_rows[slot], precision=lax.Precision.HIGHEST)
        left_side = rounded(occupied_half).reshape(NAUX, NAO * TW)
        right_side = rounded(virtual_half).reshape(NAUX, NAO * TW)
        return total + jnp.dot(left_side, right_side.T, precision=lax.Precision.HIGHEST, preferred_element_type=jnp.float32)

    total = lax.fori_loop(0, NT, one_tile, jnp.zeros((NAUX, NAUX), jnp.float32))
    return total / NAO
```

```python
import functools

import jax
import jax.numpy as jnp
from jax import lax
from jax.experimental import pallas as pl
from jax.experimental.pallas import tpu as pltpu
from jax.sharding import PartitionSpec as P

NT = 16
HALF = NT // 2 + 1
VMEM_BYTES = 60 * 1024 * 1024


def general_body(
    integrals,
    tile_mask,
    tile_owner,
    occupied_tiles,
    occupied_offsets,
    virtual_tiles,
    virtual_offsets,
):
    aux_local, basis_size, local_width = integrals.shape
    tile_width = basis_size // NT
    kcount = occupied_offsets.shape[0]
    local_tiles = local_width // tile_width
    group_index = lax.axis_index("grp")
    local_owner = lax.dynamic_slice_in_dim(tile_owner, group_index * local_tiles, local_tiles)
    matches = (local_owner[None, :, None] == jnp.arange(NT, dtype=jnp.int32)[None, None, :]).astype(
        jnp.int32
    )
    column_mask = jnp.sum(tile_mask[:, None, :] * matches, axis=2)
    blocked = integrals.reshape(aux_local, NT, tile_width, local_tiles, tile_width)
    masked = blocked * column_mask.astype(jnp.bfloat16)[None, :, None, :, None]
    masked = masked.reshape(aux_local, NT, tile_width, local_width)
    occupied_all, virtual_all = (
        lax.all_gather(occupied_tiles, ("grp", "blk"), axis=0, tiled=True),
        lax.all_gather(virtual_tiles, ("grp", "blk"), axis=0, tiled=True),
    )
    occupied_all = occupied_all.reshape(NT, kcount, tile_width, tile_width)
    virtual_all = virtual_all.reshape(NT, kcount, tile_width, tile_width)
    source_rows = (tile_owner[:, None] - occupied_offsets[None, :]) % NT
    partner_rows = (tile_owner[:, None] + virtual_offsets[None, :]) % NT
    virtual_pick = virtual_all[tile_owner]
    occupied_sum = jnp.zeros((aux_local, NT, tile_width, local_width), jnp.float32)
    virtual_sum = jnp.zeros((aux_local, local_width, NT, tile_width), jnp.float32)
    for slot in range(kcount):
        occupied_pick = occupied_all[source_rows[:, slot], slot]
        occupied_inputs = masked[:, source_rows[:, slot]]
        occupied_sum = occupied_sum + jnp.einsum(
            "tmn,ptml->ptnl", occupied_pick, occupied_inputs, preferred_element_type=jnp.float32
        )
        virtual_inputs = masked[:, partner_rows[:, slot]]
        virtual_sum = virtual_sum + jnp.einsum(
            "tnm,ptml->pltn",
            virtual_pick[:, slot],
            virtual_inputs,
            preferred_element_type=jnp.float32,
        )
    occupied_part = occupied_sum.astype(jnp.bfloat16)
    virtual_part = virtual_sum.astype(jnp.bfloat16).reshape(
        aux_local, local_tiles, tile_width, basis_size
    )
    occupied_moved = lax.all_to_all(occupied_part, "grp", split_axis=1, concat_axis=3, tiled=True)
    occupied_full, virtual_full = (
        lax.all_to_all(occupied_moved, "blk", split_axis=2, concat_axis=0, tiled=True),
        lax.all_to_all(virtual_part, "blk", split_axis=2, concat_axis=0, tiled=True),
    )
    left_side = occupied_full.reshape(occupied_full.shape[0], -1)
    right_side = virtual_full.reshape(virtual_full.shape[0], -1)
    partial_sum = jnp.einsum(
        "pe,qe->pq", left_side, right_side, preferred_element_type=jnp.float32
    ) * (1.0 / basis_size)
    total = lax.psum(partial_sum, ("grp", "blk"))
    return lax.dynamic_slice_in_dim(total, lax.axis_index("blk") * aux_local, aux_local, 0)


def order_kernel(row_ref, aux_ref, integrals_ref, mask_ref, out_ref):
    out_ref[...] = integrals_ref[...] * mask_ref[0]


def ordered_rows(integrals, row_of, aux_of, mask_rows):
    aux_local, basis_size, width = integrals.shape
    tile = basis_size // NT
    return pl.pallas_call(
        order_kernel,
        grid_spec=pltpu.PrefetchScalarGridSpec(
            num_scalar_prefetch=2,
            grid=(NT, aux_local),
            in_specs=[
                pl.BlockSpec((1, 1, tile, width), lambda r, d, row, aux: (aux[d], row[r], 0, 0)),
                pl.BlockSpec((1, 1, width), lambda r, d, row, aux: (r, 0, 0)),
            ],
            out_specs=pl.BlockSpec((1, 1, tile, width), lambda r, d, row, aux: (d, r, 0, 0)),
        ),
        out_shape=jax.ShapeDtypeStruct((aux_local, NT, tile, width), jnp.bfloat16),
        name="ordered_rows",
    )(row_of, aux_of, integrals.reshape(aux_local, NT, tile, width), mask_rows)


def pair_kernel(row_ref, integrals_ref, mask_ref, out_ref):
    parts, aux_local = out_ref.shape[0], out_ref.shape[1]
    rows = out_ref.shape[3]
    values = integrals_ref[:, 0] * mask_ref[0]
    for part in range(parts):
        out_ref[part, :, 0] = values[:, part * rows : (part + 1) * rows]


def pair_tiles(integrals, row_of, mask_rows, parts):
    aux_local, basis_size, width = integrals.shape
    tile = basis_size // NT
    columns = width // tile
    rows = tile // parts
    return pl.pallas_call(
        pair_kernel,
        grid_spec=pltpu.PrefetchScalarGridSpec(
            num_scalar_prefetch=1,
            grid=(columns, HALF),
            in_specs=[
                pl.BlockSpec((aux_local, 1, tile, tile), lambda c, d, row: (0, row[c + d], 0, c)),
                pl.BlockSpec((1, 1, tile), lambda c, d, row: (c + d, 0, c)),
            ],
            out_specs=pl.BlockSpec(
                (parts, aux_local, 1, rows, tile), lambda c, d, row: (0, 0, c * HALF + d, 0, 0)
            ),
        ),
        out_shape=jax.ShapeDtypeStruct(
            (parts, aux_local, columns * HALF, rows, tile), jnp.bfloat16
        ),
        name="pair_tiles",
    )(row_of, integrals.reshape(aux_local, NT, tile, width), mask_rows)


def product_kernel(
    kcount,
    parts,
    group_ref,
    occ_slot_ref,
    occ_tile_ref,
    virt_slot_ref,
    virt_tile_ref,
    own_ref,
    near_ref,
    across_ref,
    far_ref,
    green_ref,
    out_ref,
    full,
    half,
    panel,
    folded,
):
    width = own_ref.shape[2]
    tile = own_ref.shape[1]
    columns = width // tile
    planes = NT // columns

    def block(row, column, values):
        full[row * width : (row + 1) * width, column * width : (column + 1) * width] = values

    def both(row, column, values):
        block(row, column, values)
        block(column, row, values.T)

    def square(ref, at):
        return ref[at * columns : (at + 1) * columns].reshape(width, width)

    block(0, 0, square(own_ref, 0))
    for plane in range(1, planes):
        both(plane, 0, square(own_ref, plane))
    block(1, 1, square(near_ref, 0))
    both(2, 1, square(near_ref, 1))
    block(2, 2, square(across_ref, 0))
    both(3, 2, square(across_ref, 1))
    block(3, 3, square(far_ref, 0))
    both(1, 3, square(far_ref, 1))

    folded[...] = jnp.zeros_like(folded)

    @pl.loop(0, NT)
    def _(r):
        left = jnp.concatenate(
            [green_ref[occ_tile_ref[r * kcount + k]] for k in range(kcount)], axis=1
        )
        starts = [pl.multiple_of(occ_slot_ref[r * kcount + k] * tile, tile) for k in range(kcount)]
        for at in range(planes):
            right = jnp.concatenate(
                [full[pl.ds(start, tile), at * width : (at + 1) * width] for start in starts],
                axis=0,
            )
            values = jnp.dot(left, right, preferred_element_type=jnp.float32)
            values = values.astype(jnp.bfloat16)
            for c in range(columns):
                half[at * columns + c, pl.ds(pl.multiple_of(r * tile, tile), tile), :] = values[
                    :, c * tile : (c + 1) * tile
                ]

    @pl.loop(0, NT)
    def _(s):
        right = jnp.concatenate(
            [green_ref[virt_tile_ref[s * kcount + k]] for k in range(kcount)], axis=0
        )
        slots = [virt_slot_ref[s * kcount + k] for k in range(kcount)]
        for at in range(planes):
            left = jnp.concatenate(
                [half[slot, at * width : (at + 1) * width, :] for slot in slots], axis=1
            )
            panel[at * width : (at + 1) * width, :] = jnp.dot(
                left, right, preferred_element_type=jnp.float32
            )
        for d in range(NT):
            r = lax.rem(s + d, NT)
            values = panel[pl.ds(pl.multiple_of(r * tile, tile), tile), :]
            if d < HALF:
                folded[s, d] += values
            else:
                folded[r, NT - d] += values.T

    rows = tile // parts

    @pl.loop(0, planes)
    def _(plane):
        away = lax.rem(plane - group_ref[0] + planes, planes)

        @pl.loop(0, columns)
        def _(c):
            for d in range(HALF):
                values = folded[away * columns + c, d].astype(jnp.bfloat16)
                for part in range(parts):
                    out_ref[plane * parts + part, c * HALF + d] = values[
                        part * rows : (part + 1) * rows
                    ]


def folded_product(tables, own, near, across, far, greens, planes, parts):
    tile, width = own.shape[1:]
    columns = width // tile
    basis = NT * tile
    kcount = tables[1].shape[0] // NT
    vmem = pl.BlockSpec(memory_space=pltpu.VMEM)
    smem = pl.BlockSpec(memory_space=pltpu.SMEM)
    return pl.pallas_call(
        functools.partial(product_kernel, kcount, parts),
        in_specs=[smem] * 5 + [vmem] * 5,
        out_specs=vmem,
        out_shape=jax.ShapeDtypeStruct(
            (planes * parts, columns * HALF, tile // parts, tile), jnp.bfloat16
        ),
        scratch_shapes=[
            pltpu.VMEM((basis, basis), jnp.bfloat16),
            pltpu.VMEM((NT, basis, tile), jnp.bfloat16),
            pltpu.VMEM((basis, tile), jnp.float32),
            pltpu.VMEM((NT, HALF, tile, tile), jnp.float32),
        ],
        compiler_params=pltpu.CompilerParams(vmem_limit_bytes=VMEM_BYTES),
        name="folded_product",
    )(*tables, own, near, across, far, greens)


def folded_body(
    integrals,
    tile_mask,
    tile_owner,
    occupied_tiles,
    occupied_offsets,
    virtual_tiles,
    virtual_offsets,
):
    aux_local, basis_size, width = integrals.shape
    tile = basis_size // NT
    columns = width // tile
    planes, parts = lax.axis_size("grp"), lax.axis_size("blk")
    kcount = occupied_offsets.shape[0]
    group = lax.axis_index("grp")

    row_of = jnp.roll(tile_owner, -group * columns)
    slots = jnp.zeros((NT,), jnp.int32).at[row_of].set(jnp.arange(NT, dtype=jnp.int32))
    mask_rows = jnp.repeat(tile_mask[row_of][:, row_of[:columns]], tile, axis=1)
    mask_rows = mask_rows.astype(jnp.bfloat16)[:, None, :]
    aux_of = (group - jnp.arange(aux_local, dtype=jnp.int32)) % aux_local

    greens = jnp.stack(
        [
            jnp.swapaxes(occupied_tiles.reshape(-1, tile, tile), 1, 2),
            virtual_tiles.reshape(-1, tile, tile),
        ]
    )
    held = greens.shape[1]
    greens = lax.all_gather(greens, ("grp", "blk"), axis=0, tiled=False)
    greens = greens.reshape(-1, tile, tile)

    ordered = ordered_rows(integrals, row_of, aux_of, mask_rows)
    moved = []
    for d in range(1, planes):
        first = 1 if d < planes - 1 else 2
        sent = jnp.concatenate(
            [ordered[d, :columns], ordered[d, first * columns : (first + 1) * columns]]
        )
        moved.append(
            lax.ppermute(sent, "grp", [(h, (h - d) % planes) for h in range(planes)])
        )
    pairs = pair_tiles(integrals, row_of, mask_rows, parts)
    pairs = lax.all_to_all(pairs, "blk", split_axis=0, concat_axis=0, tiled=True)

    def table(offsets, which):
        natural = (row_of[:, None] - offsets[None, :]) % NT
        flat = natural * kcount + jnp.arange(kcount, dtype=jnp.int32)[None, :]
        at = (flat // held) * (2 * held) + which * held + flat % held
        return slots[natural].reshape(-1), at.reshape(-1)

    tables = (group[None].astype(jnp.int32),) + table(occupied_offsets, 0) + table(virtual_offsets, 1)
    folded = folded_product(tables, ordered[0], *moved, greens, planes, parts)
    folded = lax.all_to_all(folded, ("grp", "blk"), split_axis=0, concat_axis=0, tiled=True)

    partial_sum = jnp.einsum(
        "pe,qe->pq",
        folded.reshape(planes * parts, -1),
        pairs.reshape(parts * aux_local, -1),
        preferred_element_type=jnp.float32,
    ) * (1.0 / basis_size)
    partial_sum = partial_sum.reshape(planes, parts, -1).swapaxes(0, 1)
    spread = jnp.broadcast_to(partial_sum[None], (planes,) + partial_sum.shape)
    spread = spread.reshape((planes * parts,) + partial_sum.shape[1:])
    spread = lax.all_to_all(spread, ("grp", "blk"), split_axis=0, concat_axis=0, tiled=True)
    return jnp.sum(spread, axis=0)


def solution(mesh):
    planes, parts = mesh.shape["grp"], mesh.shape["blk"]

    def body(*args):
        aux_local, basis_size, width = args[0].shape
        tile = basis_size // NT
        fits = aux_local == planes == 4 and width % tile == 0 and tile % (16 * parts) == 0
        return (folded_body if fits else general_body)(*args)

    in_specs = (
        P("blk", None, "grp"),
        P(),
        P(),
        P(("grp", "blk"), None),
        P(),
        P(("grp", "blk"), None),
        P(),
    )
    out_specs = P("blk", None)
    return jax.shard_map(body, mesh=mesh, in_specs=in_specs, out_specs=out_specs, check_vma=False)
```

```python
import functools

import jax
import jax.numpy as jnp
from jax import lax
from jax.experimental import pallas as pl
from jax.experimental.pallas import tpu as pltpu
from jax.sharding import PartitionSpec as P

NT = 16
CHUNKS = ((0, NT // 2, 1), (2, 3, 4, 5, 6, 7))
OFFSETS = CHUNKS[0] + CHUNKS[1]
VMEM_BYTES = 60 * 1024 * 1024


def general_body(
    integrals,
    tile_mask,
    tile_owner,
    occupied_tiles,
    occupied_offsets,
    virtual_tiles,
    virtual_offsets,
):
    aux_local, basis_size, local_width = integrals.shape
    tile_width = basis_size // NT
    kcount = occupied_offsets.shape[0]
    local_tiles = local_width // tile_width
    group_index = lax.axis_index("grp")
    local_owner = lax.dynamic_slice_in_dim(tile_owner, group_index * local_tiles, local_tiles)
    matches = (local_owner[None, :, None] == jnp.arange(NT, dtype=jnp.int32)[None, None, :]).astype(
        jnp.int32
    )
    column_mask = jnp.sum(tile_mask[:, None, :] * matches, axis=2)
    blocked = integrals.reshape(aux_local, NT, tile_width, local_tiles, tile_width)
    masked = blocked * column_mask.astype(jnp.bfloat16)[None, :, None, :, None]
    masked = masked.reshape(aux_local, NT, tile_width, local_width)
    occupied_all, virtual_all = (
        lax.all_gather(occupied_tiles, ("grp", "blk"), axis=0, tiled=True),
        lax.all_gather(virtual_tiles, ("grp", "blk"), axis=0, tiled=True),
    )
    occupied_all = occupied_all.reshape(NT, kcount, tile_width, tile_width)
    virtual_all = virtual_all.reshape(NT, kcount, tile_width, tile_width)
    source_rows = (tile_owner[:, None] - occupied_offsets[None, :]) % NT
    partner_rows = (tile_owner[:, None] + virtual_offsets[None, :]) % NT
    virtual_pick = virtual_all[tile_owner]
    occupied_sum = jnp.zeros((aux_local, NT, tile_width, local_width), jnp.float32)
    virtual_sum = jnp.zeros((aux_local, local_width, NT, tile_width), jnp.float32)
    for slot in range(kcount):
        occupied_pick = occupied_all[source_rows[:, slot], slot]
        occupied_inputs = masked[:, source_rows[:, slot]]
        occupied_sum = occupied_sum + jnp.einsum(
            "tmn,ptml->ptnl", occupied_pick, occupied_inputs, preferred_element_type=jnp.float32
        )
        virtual_inputs = masked[:, partner_rows[:, slot]]
        virtual_sum = virtual_sum + jnp.einsum(
            "tnm,ptml->pltn",
            virtual_pick[:, slot],
            virtual_inputs,
            preferred_element_type=jnp.float32,
        )
    occupied_part = occupied_sum.astype(jnp.bfloat16)
    virtual_part = virtual_sum.astype(jnp.bfloat16).reshape(
        aux_local, local_tiles, tile_width, basis_size
    )
    occupied_moved = lax.all_to_all(occupied_part, "grp", split_axis=1, concat_axis=3, tiled=True)
    occupied_full, virtual_full = (
        lax.all_to_all(occupied_moved, "blk", split_axis=2, concat_axis=0, tiled=True),
        lax.all_to_all(virtual_part, "blk", split_axis=2, concat_axis=0, tiled=True),
    )
    left_side = occupied_full.reshape(occupied_full.shape[0], -1)
    right_side = virtual_full.reshape(virtual_full.shape[0], -1)
    partial_sum = jnp.einsum(
        "pe,qe->pq", left_side, right_side, preferred_element_type=jnp.float32
    ) * (1.0 / basis_size)
    total = lax.psum(partial_sum, ("grp", "blk"))
    return lax.dynamic_slice_in_dim(total, lax.axis_index("blk") * aux_local, aux_local, 0)


def place(refs, tile_row, column):
    owner_ref, mask_ref = refs
    return mask_ref[tile_row * NT + owner_ref[column]]


def masked_tile(values, kept):
    return values * jnp.full(values.shape, kept, jnp.int32).astype(values.dtype)


def picked_kernel(columns, planes_of, where_ref, owner_ref, mask_ref, *refs):
    inputs, out_ref = refs[:-1], refs[-1]
    tile = out_ref.shape[1]
    group = where_ref[0]
    row_plane = planes_of(pl.program_id(0)) ^ group
    for q in range(columns):
        tile_row = owner_ref[row_plane * columns + q]
        for c in range(columns):
            lanes = slice(c * tile, (c + 1) * tile)
            kept = place((owner_ref, mask_ref), tile_row, group * columns + c)
            out_ref[q, :, lanes] = masked_tile(inputs[q][0, 0, :, lanes], kept)


def picked_rows(scalars, integrals, away, row_planes):
    aux_local, basis_size, width = integrals.shape
    tile = basis_size // NT
    columns = width // tile

    def planes_of(i):
        return sum(jnp.where(i == at, plane, 0) for at, plane in enumerate(row_planes))

    def row_map(q):
        def index(i, where, owner, mask):
            plane = planes_of(i) ^ where[0]
            return (where[0] ^ away, owner[plane * columns + q], 0, 0)

        return index

    return pl.pallas_call(
        functools.partial(picked_kernel, columns, planes_of),
        grid_spec=pltpu.PrefetchScalarGridSpec(
            num_scalar_prefetch=3,
            grid=(len(row_planes),),
            in_specs=[pl.BlockSpec((1, 1, tile, width), row_map(q)) for q in range(columns)],
            out_specs=pl.BlockSpec((columns, tile, width), lambda i, *_: (i, 0, 0)),
        ),
        out_shape=jax.ShapeDtypeStruct((len(row_planes) * columns, tile, width), jnp.bfloat16),
        compiler_params=pltpu.CompilerParams(vmem_limit_bytes=VMEM_BYTES),
        cost_estimate=pl.CostEstimate(flops=0, bytes_accessed=0, transcendentals=0),
        name="picked_rows",
    )(*scalars, *([integrals.reshape(aux_local, NT, tile, width)] * columns))


def offset_at(i):
    return sum(jnp.where(i == at, offset, 0) for at, offset in enumerate(OFFSETS))


def pair_kernel(columns, where_ref, owner_ref, mask_ref, *refs):
    inputs, out_refs = refs[:columns], refs[columns:]
    rows = out_refs[0].shape[3]
    first = where_ref[0] * columns
    for c in range(columns):
        tile_row = owner_ref[lax.rem(first + c + offset_at(pl.program_id(0)), NT)]
        kept = place((owner_ref, mask_ref), tile_row, first + c)
        for part, out_ref in enumerate(out_refs):
            start = pl.multiple_of((part ^ where_ref[1]) * rows, rows)
            out_ref[:, 0, c] = masked_tile(inputs[c][:, 0, pl.ds(start, rows), :], kept)


def pair_tiles(scalars, integrals, parts):
    aux_local, basis_size, width = integrals.shape
    tile = basis_size // NT
    columns = width // tile
    rows = tile // parts

    def row_map(c):
        def index(d, where, owner, mask):
            return (0, owner[lax.rem(where[0] * columns + c + offset_at(d), NT)], 0, c)

        return index

    return pl.pallas_call(
        functools.partial(pair_kernel, columns),
        grid_spec=pltpu.PrefetchScalarGridSpec(
            num_scalar_prefetch=3,
            grid=(len(OFFSETS),),
            in_specs=[
                pl.BlockSpec((aux_local, 1, tile, tile), row_map(c)) for c in range(columns)
            ],
            out_specs=[
                pl.BlockSpec((aux_local, 1, columns, rows, tile), lambda d, *_: (0, d, 0, 0, 0))
            ]
            * parts,
        ),
        out_shape=[
            jax.ShapeDtypeStruct((aux_local, len(OFFSETS), columns, rows, tile), jnp.bfloat16)
        ]
        * parts,
        compiler_params=pltpu.CompilerParams(vmem_limit_bytes=VMEM_BYTES),
        cost_estimate=pl.CostEstimate(flops=0, bytes_accessed=0, transcendentals=0),
        name="pair_tiles",
    )(*scalars, *([integrals.reshape(aux_local, NT, tile, width)] * columns))


def start_all(copies):
    for copy in copies:
        copy.start()


def wait_all(copies):
    for copy in copies:
        copy.wait()


def green_copies(green_refs, which, green, sems):
    planes, held = green_refs[0].shape[0], green_refs[0].shape[2]
    copies = []
    for part, ref in enumerate(green_refs):
        for plane in range(planes):
            at = part * planes + plane
            copies.append(
                pltpu.make_async_copy(
                    ref.at[plane, which], green.at[pl.ds(at * held, held)], sems.at[at]
                )
            )
    return copies


def occupied_columns(kcount, column_blocks, slot_ref, tile_ref, block_refs, green, full, half):
    tile = green.shape[1]
    width = full.shape[1] // len(column_blocks)
    columns = width // tile
    for at, blocks in enumerate(column_blocks):
        for plane, (ref, first, turned) in enumerate(blocks):
            values = block_refs[ref][first * columns : (first + 1) * columns]
            values = values.reshape(width, width)
            full[plane * width : (plane + 1) * width, at * width : (at + 1) * width] = (
                values.T if turned else values
            )

    @pl.loop(0, NT)
    def _(r):
        left = jnp.concatenate([green[tile_ref[r * kcount + k]] for k in range(kcount)], axis=1)
        starts = [pl.multiple_of(slot_ref[r * kcount + k] * tile, tile) for k in range(kcount)]
        rows = pl.ds(pl.multiple_of(r * tile, tile), tile)
        for at in range(len(column_blocks)):
            right = jnp.concatenate(
                [full[pl.ds(start, tile), at * width : (at + 1) * width] for start in starts],
                axis=0,
            )
            values = jnp.dot(left, right, preferred_element_type=jnp.float32)
            values = values.astype(jnp.bfloat16)
            for c in range(columns):
                half[at * columns + c, rows, :] = values[:, c * tile : (c + 1) * tile]


def folded_pairs(kcount, columns, offsets, group, slot_ref, tile_ref, green, half, folded, out_ref):
    tile = green.shape[1]
    folded[...] = jnp.zeros_like(folded)
    pieces = [(at, d, False) for at, d in enumerate(offsets)]
    pieces += [(at, NT - d, True) for at, d in enumerate(offsets) if 0 < d < NT // 2]

    @pl.loop(0, NT)
    def _(s):
        right = jnp.concatenate([green[tile_ref[s * kcount + k]] for k in range(kcount)], axis=0)
        slots = [slot_ref[s * kcount + k] for k in range(kcount)]
        for first in range(0, len(pieces), 4):
            some = pieces[first : first + 4]
            rows = [lax.rem(s + shift, NT) for _, shift, _ in some]
            left = []
            for r in rows:
                start = ((r // columns) ^ group) * columns + lax.rem(r, columns)
                start = pl.multiple_of(start * tile, tile)
                left.append(
                    jnp.concatenate([half[slot, pl.ds(start, tile), :] for slot in slots], axis=1)
                )
            values = jnp.dot(
                jnp.concatenate(left, axis=0), right, preferred_element_type=jnp.float32
            )
            for place_at, ((at, _, turned), r) in enumerate(zip(some, rows)):
                piece = values[place_at * tile : (place_at + 1) * tile]
                if turned:
                    folded[r, at] += piece.T
                else:
                    folded[s, at] += piece

    rows = out_ref.shape[3]
    parts = tile // rows

    @pl.loop(0, NT // columns)
    def _(plane):
        @pl.loop(0, columns)
        def _(c):
            for at in range(len(offsets)):
                values = folded[plane * columns + c, at].astype(jnp.bfloat16)
                for part in range(parts):
                    out_ref[plane * parts + part, at, c] = values[part * rows : (part + 1) * rows]


def early_kernel(kcount, column_blocks, parts, slot_ref, tile_ref, *refs):
    green_refs, refs = refs[:parts], refs[parts:]
    block_refs, (half_ref, green, full, sems) = refs[:-4], refs[-4:]
    copies = green_copies(green_refs, 0, green, sems)
    start_all(copies)
    wait_all(copies)
    occupied_columns(kcount, column_blocks, slot_ref, tile_ref, block_refs, green, full, half_ref)


def last_kernel(
    kcount, columns, column_blocks, offsets, parts, group_ref, slot_ref, tile_ref, half_slot_ref,
    virtual_tile_ref, *refs
):
    green_refs, refs = refs[:parts], refs[parts:]
    held_ref, refs = refs[0], refs[1:]
    block_refs, refs = refs[:-9], refs[-9:]
    out_ref, half_ref, green, virtual, full, half, folded, sems, others = refs
    copies = green_copies(green_refs, 0, green, sems)
    later = green_copies(green_refs, 1, virtual, others)
    count = held_ref.shape[0]
    later.append(
        pltpu.make_async_copy(held_ref, half.at[pl.ds(0, count)], others.at[others.shape[0] - 1])
    )
    start_all(copies + later)
    wait_all(copies)
    occupied_columns(kcount, column_blocks, slot_ref, tile_ref, block_refs, green, full, half_ref)
    wait_all(later)
    half[count:] = half_ref[...]
    folded_pairs(
        kcount, columns, offsets, group_ref[0], half_slot_ref, virtual_tile_ref, virtual, half,
        folded, out_ref,
    )


def rest_kernel(
    kcount, columns, offsets, parts, group_ref, half_slot_ref, virtual_tile_ref, *refs
):
    green_refs, refs = refs[:parts], refs[parts:]
    held_ref, new_ref, out_ref, virtual, half, folded, others = refs
    copies = green_copies(green_refs, 1, virtual, others)
    count = held_ref.shape[0]
    last = others.shape[0] - 2
    copies.append(pltpu.make_async_copy(held_ref, half.at[pl.ds(0, count)], others.at[last]))
    copies.append(
        pltpu.make_async_copy(
            new_ref, half.at[pl.ds(count, new_ref.shape[0])], others.at[last + 1]
        )
    )
    start_all(copies)
    wait_all(copies)
    folded_pairs(
        kcount, columns, offsets, group_ref[0], half_slot_ref, virtual_tile_ref, virtual, half,
        folded, out_ref,
    )


def kernel_call(kernel, tables, anywhere, blocks, out_shape, scratch_shapes, name, flops=0):
    return pl.pallas_call(
        kernel,
        in_specs=[pl.BlockSpec(memory_space=pltpu.SMEM)] * len(tables)
        + [pl.BlockSpec(memory_space=pl.ANY)] * len(anywhere)
        + [pl.BlockSpec(memory_space=pltpu.VMEM)] * len(blocks),
        out_specs=jax.tree.map(lambda _: pl.BlockSpec(memory_space=pltpu.VMEM), out_shape),
        out_shape=out_shape,
        scratch_shapes=scratch_shapes,
        compiler_params=pltpu.CompilerParams(vmem_limit_bytes=VMEM_BYTES),
        cost_estimate=pl.CostEstimate(flops=flops, bytes_accessed=flops // 512, transcendentals=0),
        name=name,
    )(*tables, *anywhere, *blocks)


def folded_body(
    integrals,
    tile_mask,
    tile_owner,
    occupied_tiles,
    occupied_offsets,
    virtual_tiles,
    virtual_offsets,
):
    aux_local, basis_size, width = integrals.shape
    tile = basis_size // NT
    columns = width // tile
    planes, parts = lax.axis_size("grp"), lax.axis_size("blk")
    kcount = occupied_offsets.shape[0]
    group = lax.axis_index("grp")

    part = lax.axis_index("blk")
    scalars = (
        jnp.stack([group, part]).astype(jnp.int32),
        tile_owner,
        tile_mask.reshape(-1),
    )

    def swap(values, axis, size, distance):
        return lax.ppermute(values, axis, [(at, at ^ distance) for at in range(size)])

    greens = jnp.stack(
        [
            jnp.swapaxes(occupied_tiles.reshape(-1, tile, tile), 1, 2),
            virtual_tiles.reshape(-1, tile, tile),
        ]
    )
    held = greens.shape[1]
    greens = jnp.stack([greens] + [swap(greens, "grp", planes, j) for j in range(1, planes)])
    pairs = list(pair_tiles(scalars, integrals, parts))
    for m in (2, 4):
        pairs[m] = swap(pairs[m], "blk", parts, m)
    near_off = picked_rows(scalars, integrals, 1, (3, 2))
    across = picked_rows(scalars, integrals, 2, (0, 1))

    slot = jnp.arange(NT, dtype=jnp.int32)
    ordered = jnp.zeros((NT,), jnp.int32).at[tile_owner].set(slot)
    ordered = (ordered // columns ^ group) * columns + ordered % columns
    nearby = (slot // columns ^ group) * columns + slot % columns

    def table(targets, offsets, order):
        natural = (targets[:, None] - offsets[None, :]) % NT
        flat = natural * kcount + jnp.arange(kcount, dtype=jnp.int32)[None, :]
        device = flat // held
        plane, other = device // parts ^ group, device % parts ^ part
        at = ((other * planes + plane) * held) + flat % held
        return order[natural].reshape(-1), at.reshape(-1)

    plane = ordered // columns
    halved = (plane % 2 * 2 + plane // 2) * columns + ordered % columns
    occupied_table = table(tile_owner[nearby], occupied_offsets, ordered)
    virtual_table = table(tile_owner, virtual_offsets, halved)

    greens, near_off, across, pairs = lax.optimization_barrier((greens, near_off, across, pairs))
    greens = [greens] + [swap(greens, "blk", parts, m) for m in range(2, parts, 2)]
    near_off = swap(near_off, "grp", planes, 1)
    across = swap(across, "grp", planes, 2)
    near = picked_rows(scalars, integrals, 1, (0,))
    far = picked_rows(scalars, integrals, 3, (0,))
    own = picked_rows(scalars, integrals, 0, (0, 1, 2, 3))

    greens, near_off, across, near, far, own, pairs, occupied_table, virtual_table = (
        lax.optimization_barrier(
            (greens, near_off, across, near, far, own, pairs, occupied_table, virtual_table)
        )
    )
    near = swap(near, "grp", planes, 1)
    far = swap(far, "grp", planes, 3)
    greens = [each for mine in greens for each in (mine, swap(mine, "blk", parts, 1))]
    for m in (3, 5):
        pairs[m] = swap(pairs[m], "blk", parts, m)

    where = scalars[0]

    def vmem(*shape, dtype=jnp.bfloat16):
        return pltpu.VMEM(shape, dtype)

    devices = planes * parts
    green = vmem(devices * held, tile, tile)

    def full(count):
        return vmem(basis_size, count * width)

    def half(count):
        return jax.ShapeDtypeStruct((count * columns, basis_size, tile), jnp.bfloat16)

    def folded(offsets):
        return (
            jax.ShapeDtypeStruct(
                (devices, len(offsets), columns, tile // parts, tile), jnp.bfloat16
            ),
            vmem(NT, len(offsets), tile, tile, dtype=jnp.float32),
        )

    column_blocks = (
        tuple((0, plane, False) for plane in range(planes)),
        ((0, 2, True), (1, 0, True), (2, 0, False), (2, 1, False)),
    )
    first = kernel_call(
        functools.partial(early_kernel, kcount, column_blocks, parts),
        occupied_table,
        greens,
        (own, near_off, across),
        half(2),
        [green, full(2), pltpu.SemaphoreType.DMA((devices,))],
        "early_half",
    )
    first, near, far, pairs = lax.optimization_barrier((first, near, far, pairs))
    column_blocks = (
        ((0, 1, True), (3, 0, False), (1, 0, False), (1, 1, False)),
        ((0, 3, True), (1, 1, True), (2, 1, True), (4, 0, False)),
    )
    out_shape, scratch = folded(CHUNKS[0])
    sent, second = kernel_call(
        functools.partial(last_kernel, kcount, columns, column_blocks, CHUNKS[0], parts),
        (where,) + occupied_table + virtual_table,
        [*greens, first],
        (own, near_off, across, near, far),
        (out_shape, half(2)),
        [
            green,
            green,
            full(2),
            vmem(NT, basis_size, tile),
            scratch,
            pltpu.SemaphoreType.DMA((devices,)),
            pltpu.SemaphoreType.DMA((devices + 1,)),
        ],
        "last_half_and_pairs",
    )
    sent, second, pairs = lax.optimization_barrier((sent, second, pairs))
    for m in (1, 6, 7):
        pairs[m] = swap(pairs[m], "blk", parts, m)
    out_shape, scratch = folded(CHUNKS[1])
    rest = kernel_call(
        functools.partial(rest_kernel, kcount, columns, CHUNKS[1], parts),
        (where,) + virtual_table,
        [*greens, first, second],
        (),
        out_shape,
        [
            green,
            vmem(NT, basis_size, tile),
            scratch,
            pltpu.SemaphoreType.DMA((devices + 2,)),
        ],
        "other_pairs",
        flops=2 * 14 * basis_size * kcount * tile * tile * 2,
    )

    def everyone(values):
        return lax.all_to_all(values, ("grp", "blk"), split_axis=0, concat_axis=0, tiled=True)

    sent = everyone(sent)
    sent, rest, pairs = lax.optimization_barrier((sent, rest, pairs))
    rest = everyone(rest)

    pairs = jnp.stack(pairs)
    partial_sum = 0.0
    at = 0
    for offsets, each in zip(CHUNKS, (sent, rest)):
        theirs = pairs[:, :, at : at + len(offsets)].reshape(parts * aux_local, -1)
        at += len(offsets)
        partial_sum = partial_sum + jnp.einsum(
            "pe,qe->pq", each.reshape(devices, -1), theirs, preferred_element_type=jnp.float32
        )
    partial_sum = partial_sum * (1.0 / basis_size)
    partial_sum = partial_sum.reshape(planes, parts, parts, aux_local)
    partial_sum = partial_sum[:, :, jnp.arange(parts, dtype=jnp.int32) ^ part]
    partial_sum = partial_sum.swapaxes(0, 1).reshape(1, parts, planes, -1)
    spread = jnp.broadcast_to(partial_sum, (planes,) + partial_sum.shape[1:])
    spread = everyone(spread.reshape((devices,) + partial_sum.shape[2:]))
    return jnp.sum(spread, axis=0)


def solution(mesh):
    planes, parts = mesh.shape["grp"], mesh.shape["blk"]

    def body(*args):
        aux_local, basis_size, width = args[0].shape
        tile = basis_size // NT
        fits = aux_local == planes == 4 and parts == 8 and width % tile == 0 and tile % (16 * parts) == 0
        return (folded_body if fits else general_body)(*args)

    in_specs = (
        P("blk", None, "grp"),
        P(),
        P(),
        P(("grp", "blk"), None),
        P(),
        P(("grp", "blk"), None),
        P(),
    )
    out_specs = P("blk", None)
    return jax.shard_map(body, mesh=mesh, in_specs=in_specs, out_specs=out_specs, check_vma=False)
```

```python
import functools

import jax
import jax.numpy as jnp
from jax import lax
from jax.experimental import pallas as pl
from jax.experimental.pallas import tpu as pltpu
from jax.sharding import PartitionSpec as P

NT = 16
CHUNKS = ((0, NT // 2), (1, 2, 3, 4, 5, 6, 7))
OFFSETS = CHUNKS[0] + CHUNKS[1]
PARTS = ((0, 1), (2, 3), (4, 5), (6,), (7,))
VMEM_BYTES = 60 * 1024 * 1024


def general_body(
    integrals,
    tile_mask,
    tile_owner,
    occupied_tiles,
    occupied_offsets,
    virtual_tiles,
    virtual_offsets,
):
    aux_local, basis_size, local_width = integrals.shape
    tile_width = basis_size // NT
    kcount = occupied_offsets.shape[0]
    local_tiles = local_width // tile_width
    group_index = lax.axis_index("grp")
    local_owner = lax.dynamic_slice_in_dim(tile_owner, group_index * local_tiles, local_tiles)
    matches = (local_owner[None, :, None] == jnp.arange(NT, dtype=jnp.int32)[None, None, :]).astype(
        jnp.int32
    )
    column_mask = jnp.sum(tile_mask[:, None, :] * matches, axis=2)
    blocked = integrals.reshape(aux_local, NT, tile_width, local_tiles, tile_width)
    masked = blocked * column_mask.astype(jnp.bfloat16)[None, :, None, :, None]
    masked = masked.reshape(aux_local, NT, tile_width, local_width)
    occupied_all, virtual_all = (
        lax.all_gather(occupied_tiles, ("grp", "blk"), axis=0, tiled=True),
        lax.all_gather(virtual_tiles, ("grp", "blk"), axis=0, tiled=True),
    )
    occupied_all = occupied_all.reshape(NT, kcount, tile_width, tile_width)
    virtual_all = virtual_all.reshape(NT, kcount, tile_width, tile_width)
    source_rows = (tile_owner[:, None] - occupied_offsets[None, :]) % NT
    partner_rows = (tile_owner[:, None] + virtual_offsets[None, :]) % NT
    virtual_pick = virtual_all[tile_owner]
    occupied_sum = jnp.zeros((aux_local, NT, tile_width, local_width), jnp.float32)
    virtual_sum = jnp.zeros((aux_local, local_width, NT, tile_width), jnp.float32)
    for slot in range(kcount):
        occupied_pick = occupied_all[source_rows[:, slot], slot]
        occupied_inputs = masked[:, source_rows[:, slot]]
        occupied_sum = occupied_sum + jnp.einsum(
            "tmn,ptml->ptnl", occupied_pick, occupied_inputs, preferred_element_type=jnp.float32
        )
        virtual_inputs = masked[:, partner_rows[:, slot]]
        virtual_sum = virtual_sum + jnp.einsum(
            "tnm,ptml->pltn",
            virtual_pick[:, slot],
            virtual_inputs,
            preferred_element_type=jnp.float32,
        )
    occupied_part = occupied_sum.astype(jnp.bfloat16)
    virtual_part = virtual_sum.astype(jnp.bfloat16).reshape(
        aux_local, local_tiles, tile_width, basis_size
    )
    occupied_moved = lax.all_to_all(occupied_part, "grp", split_axis=1, concat_axis=3, tiled=True)
    occupied_full, virtual_full = (
        lax.all_to_all(occupied_moved, "blk", split_axis=2, concat_axis=0, tiled=True),
        lax.all_to_all(virtual_part, "blk", split_axis=2, concat_axis=0, tiled=True),
    )
    left_side = occupied_full.reshape(occupied_full.shape[0], -1)
    right_side = virtual_full.reshape(virtual_full.shape[0], -1)
    partial_sum = jnp.einsum(
        "pe,qe->pq", left_side, right_side, preferred_element_type=jnp.float32
    ) * (1.0 / basis_size)
    total = lax.psum(partial_sum, ("grp", "blk"))
    return lax.dynamic_slice_in_dim(total, lax.axis_index("blk") * aux_local, aux_local, 0)


def place(refs, tile_row, column):
    owner_ref, mask_ref = refs
    return mask_ref[tile_row * NT + owner_ref[column]]


def masked_tile(values, kept):
    return values * jnp.full(values.shape, kept, jnp.int32).astype(values.dtype)


def picked_kernel(columns, planes_of, where_ref, owner_ref, mask_ref, *refs):
    inputs, out_ref = refs[:-1], refs[-1]
    tile = out_ref.shape[1]
    group = where_ref[0]
    row_plane = planes_of(pl.program_id(0)) ^ group
    for q in range(columns):
        tile_row = owner_ref[row_plane * columns + q]
        for c in range(columns):
            lanes = slice(c * tile, (c + 1) * tile)
            kept = place((owner_ref, mask_ref), tile_row, group * columns + c)
            out_ref[q, :, lanes] = masked_tile(inputs[q][0, 0, :, lanes], kept)


def triangle(columns):
    return [(q, c) for q in range(columns) for c in range(q + 1)]


def picked_square_kernel(columns, where_ref, owner_ref, mask_ref, *refs):
    inputs, out_ref = refs[:-1], refs[-1]
    tile = out_ref.shape[1]
    first = where_ref[0] * columns
    for at, (q, c) in enumerate(triangle(columns)):
        kept = place((owner_ref, mask_ref), owner_ref[first + q], first + c)
        out_ref[at] = masked_tile(inputs[q][0, 0, :, c * tile : (c + 1) * tile], kept)


def picked_square(scalars, integrals, away):
    aux_local, basis_size, width = integrals.shape
    tile = basis_size // NT
    columns = width // tile
    count = len(triangle(columns))

    def row_map(q):
        def index(i, where, owner, mask):
            return (where[0] ^ away, owner[where[0] * columns + q], 0, 0)

        return index

    return pl.pallas_call(
        functools.partial(picked_square_kernel, columns),
        grid_spec=pltpu.PrefetchScalarGridSpec(
            num_scalar_prefetch=3,
            grid=(1,),
            in_specs=[pl.BlockSpec((1, 1, tile, width), row_map(q)) for q in range(columns)],
            out_specs=pl.BlockSpec((count, tile, tile), lambda i, *_: (0, 0, 0)),
        ),
        out_shape=jax.ShapeDtypeStruct((count, tile, tile), jnp.bfloat16),
        compiler_params=pltpu.CompilerParams(vmem_limit_bytes=VMEM_BYTES),
        cost_estimate=pl.CostEstimate(flops=0, bytes_accessed=0, transcendentals=0),
        name="picked_square",
    )(*scalars, *([integrals.reshape(aux_local, NT, tile, width)] * columns))


def picked_rows(scalars, integrals, away, row_planes):
    aux_local, basis_size, width = integrals.shape
    tile = basis_size // NT
    columns = width // tile

    def planes_of(i):
        return sum(jnp.where(i == at, plane, 0) for at, plane in enumerate(row_planes))

    def row_map(q):
        def index(i, where, owner, mask):
            plane = planes_of(i) ^ where[0]
            return (where[0] ^ away, owner[plane * columns + q], 0, 0)

        return index

    return pl.pallas_call(
        functools.partial(picked_kernel, columns, planes_of),
        grid_spec=pltpu.PrefetchScalarGridSpec(
            num_scalar_prefetch=3,
            grid=(len(row_planes),),
            in_specs=[pl.BlockSpec((1, 1, tile, width), row_map(q)) for q in range(columns)],
            out_specs=pl.BlockSpec((columns, tile, width), lambda i, *_: (i, 0, 0)),
        ),
        out_shape=jax.ShapeDtypeStruct((len(row_planes) * columns, tile, width), jnp.bfloat16),
        compiler_params=pltpu.CompilerParams(vmem_limit_bytes=VMEM_BYTES),
        cost_estimate=pl.CostEstimate(flops=0, bytes_accessed=0, transcendentals=0),
        name="picked_rows",
    )(*scalars, *([integrals.reshape(aux_local, NT, tile, width)] * columns))


def offset_at(i):
    return sum(jnp.where(i == at, offset, 0) for at, offset in enumerate(OFFSETS))


def pair_kernel(columns, where_ref, owner_ref, mask_ref, *refs):
    inputs, out_refs = refs[:columns], refs[columns:]
    rows = out_refs[0].shape[4]
    first = where_ref[0] * columns
    for c in range(columns):
        tile_row = owner_ref[lax.rem(first + c + offset_at(pl.program_id(0)), NT)]
        kept = place((owner_ref, mask_ref), tile_row, first + c)
        for out_ref, some in zip(out_refs, PARTS):
            for at, part in enumerate(some):
                start = pl.multiple_of((part ^ where_ref[1]) * rows, rows)
                out_ref[at, :, 0, c] = masked_tile(inputs[c][:, 0, pl.ds(start, rows), :], kept)


def pair_tiles(scalars, integrals, parts):
    aux_local, basis_size, width = integrals.shape
    tile = basis_size // NT
    columns = width // tile
    rows = tile // parts

    def row_map(c):
        def index(d, where, owner, mask):
            return (0, owner[lax.rem(where[0] * columns + c + offset_at(d), NT)], 0, c)

        return index

    return pl.pallas_call(
        functools.partial(pair_kernel, columns),
        grid_spec=pltpu.PrefetchScalarGridSpec(
            num_scalar_prefetch=3,
            grid=(len(OFFSETS),),
            in_specs=[
                pl.BlockSpec((aux_local, 1, tile, tile), row_map(c)) for c in range(columns)
            ],
            out_specs=[
                pl.BlockSpec(
                    (len(some), aux_local, 1, columns, rows, tile),
                    lambda d, *_: (0, 0, d, 0, 0, 0),
                )
                for some in PARTS
            ],
        ),
        out_shape=[
            jax.ShapeDtypeStruct(
                (len(some), aux_local, len(OFFSETS), columns, rows, tile), jnp.bfloat16
            )
            for some in PARTS
        ],
        compiler_params=pltpu.CompilerParams(vmem_limit_bytes=VMEM_BYTES),
        cost_estimate=pl.CostEstimate(flops=0, bytes_accessed=0, transcendentals=0),
        name="pair_tiles",
    )(*scalars, *([integrals.reshape(aux_local, NT, tile, width)] * columns))


def start_all(copies):
    for copy in copies:
        copy.start()


def wait_all(copies):
    for copy in copies:
        copy.wait()


def green_copies(green_refs, which, green, sems):
    copies = []
    for ref in green_refs:
        held = ref.shape[2]
        for plane in range(ref.shape[0]):
            at = len(copies)
            copies.append(
                pltpu.make_async_copy(
                    ref.at[plane, which], green.at[pl.ds(at * held, held)], sems.at[at]
                )
            )
    return copies


def occupied_columns(kcount, column_blocks, slot_ref, tile_ref, block_refs, green, full, half):
    tile = green.shape[1]
    width = full.shape[1] // len(column_blocks)
    columns = width // tile
    for at, blocks in enumerate(column_blocks):
        for plane, (ref, first, turned) in enumerate(blocks):
            if first is None:
                for i, (q, c) in enumerate(triangle(columns)):
                    row, column = plane * width + q * tile, at * width + c * tile
                    values = block_refs[ref][i]
                    full[row : row + tile, column : column + tile] = values
                    if q != c:
                        row, column = plane * width + c * tile, at * width + q * tile
                        full[row : row + tile, column : column + tile] = values.T
                continue
            values = block_refs[ref][first * columns : (first + 1) * columns]
            values = values.reshape(width, width)
            full[plane * width : (plane + 1) * width, at * width : (at + 1) * width] = (
                values.T if turned else values
            )

    @pl.loop(0, NT)
    def _(r):
        left = jnp.concatenate([green[tile_ref[r * kcount + k]] for k in range(kcount)], axis=1)
        starts = [pl.multiple_of(slot_ref[r * kcount + k] * tile, tile) for k in range(kcount)]
        rows = pl.ds(pl.multiple_of(r * tile, tile), tile)
        for at in range(len(column_blocks)):
            right = jnp.concatenate(
                [full[pl.ds(start, tile), at * width : (at + 1) * width] for start in starts],
                axis=0,
            )
            values = jnp.dot(left, right, preferred_element_type=jnp.float32)
            values = values.astype(jnp.bfloat16)
            for c in range(columns):
                half[at * columns + c, rows, :] = values[:, c * tile : (c + 1) * tile]


def folded_pairs(kcount, columns, offsets, group, slot_ref, tile_ref, green, half, folded, out_ref):
    tile = green.shape[1]
    folded[...] = jnp.zeros_like(folded)
    pieces = [(at, d, False) for at, d in enumerate(offsets)]
    pieces += [(at, NT - d, True) for at, d in enumerate(offsets) if 0 < d < NT // 2]

    @pl.loop(0, NT)
    def _(s):
        right = jnp.concatenate([green[tile_ref[s * kcount + k]] for k in range(kcount)], axis=0)
        slots = [slot_ref[s * kcount + k] for k in range(kcount)]
        for first in range(0, len(pieces), 4):
            some = pieces[first : first + 4]
            rows = [lax.rem(s + shift, NT) for _, shift, _ in some]
            left = []
            for r in rows:
                start = ((r // columns) ^ group) * columns + lax.rem(r, columns)
                start = pl.multiple_of(start * tile, tile)
                left.append(
                    jnp.concatenate([half[slot, pl.ds(start, tile), :] for slot in slots], axis=1)
                )
            values = jnp.dot(
                jnp.concatenate(left, axis=0), right, preferred_element_type=jnp.float32
            )
            for place_at, ((at, _, turned), r) in enumerate(zip(some, rows)):
                piece = values[place_at * tile : (place_at + 1) * tile]
                if turned:
                    folded[r, at] += piece.T
                else:
                    folded[s, at] += piece

    rows = out_ref.shape[3]
    parts = tile // rows

    @pl.loop(0, NT // columns)
    def _(plane):
        @pl.loop(0, columns)
        def _(c):
            for at in range(len(offsets)):
                values = folded[plane * columns + c, at].astype(jnp.bfloat16)
                for part in range(parts):
                    out_ref[plane * parts + part, at, c] = values[part * rows : (part + 1) * rows]


def early_kernel(kcount, column_blocks, parts, slot_ref, tile_ref, *refs):
    green_refs, refs = refs[:parts], refs[parts:]
    block_refs, (half_ref, green, full, sems) = refs[:-4], refs[-4:]
    copies = green_copies(green_refs, 0, green, sems)
    start_all(copies)
    wait_all(copies)
    occupied_columns(kcount, column_blocks, slot_ref, tile_ref, block_refs, green, full, half_ref)


def last_kernel(
    kcount, columns, column_blocks, offsets, parts, group_ref, slot_ref, tile_ref, half_slot_ref,
    virtual_tile_ref, *refs
):
    green_refs, refs = refs[:parts], refs[parts:]
    held_ref, refs = refs[0], refs[1:]
    block_refs, refs = refs[:-9], refs[-9:]
    out_ref, half_ref, green, virtual, full, half, folded, sems, others = refs
    copies = green_copies(green_refs, 0, green, sems)
    later = green_copies(green_refs, 1, virtual, others)
    count = held_ref.shape[0]
    later.append(
        pltpu.make_async_copy(held_ref, half.at[pl.ds(0, count)], others.at[others.shape[0] - 1])
    )
    start_all(copies + later)
    wait_all(copies)
    occupied_columns(kcount, column_blocks, slot_ref, tile_ref, block_refs, green, full, half_ref)
    wait_all(later)
    half[count:] = half_ref[...]
    folded_pairs(
        kcount, columns, offsets, group_ref[0], half_slot_ref, virtual_tile_ref, virtual, half,
        folded, out_ref,
    )


def rest_kernel(
    kcount, columns, offsets, parts, group_ref, half_slot_ref, virtual_tile_ref, *refs
):
    green_refs, refs = refs[:parts], refs[parts:]
    held_ref, new_ref, out_ref, virtual, half, folded, others = refs
    copies = green_copies(green_refs, 1, virtual, others)
    count = held_ref.shape[0]
    last = others.shape[0] - 2
    copies.append(pltpu.make_async_copy(held_ref, half.at[pl.ds(0, count)], others.at[last]))
    copies.append(
        pltpu.make_async_copy(
            new_ref, half.at[pl.ds(count, new_ref.shape[0])], others.at[last + 1]
        )
    )
    start_all(copies)
    wait_all(copies)
    folded_pairs(
        kcount, columns, offsets, group_ref[0], half_slot_ref, virtual_tile_ref, virtual, half,
        folded, out_ref,
    )


def kernel_call(kernel, tables, anywhere, blocks, out_shape, scratch_shapes, name, flops=0):
    return pl.pallas_call(
        kernel,
        in_specs=[pl.BlockSpec(memory_space=pltpu.SMEM)] * len(tables)
        + [pl.BlockSpec(memory_space=pl.ANY)] * len(anywhere)
        + [pl.BlockSpec(memory_space=pltpu.VMEM)] * len(blocks),
        out_specs=jax.tree.map(lambda _: pl.BlockSpec(memory_space=pltpu.VMEM), out_shape),
        out_shape=out_shape,
        scratch_shapes=scratch_shapes,
        compiler_params=pltpu.CompilerParams(vmem_limit_bytes=VMEM_BYTES),
        cost_estimate=pl.CostEstimate(flops=flops, bytes_accessed=flops // 512, transcendentals=0),
        name=name,
    )(*tables, *anywhere, *blocks)


def folded_body(
    integrals,
    tile_mask,
    tile_owner,
    occupied_tiles,
    occupied_offsets,
    virtual_tiles,
    virtual_offsets,
):
    aux_local, basis_size, width = integrals.shape
    tile = basis_size // NT
    columns = width // tile
    planes, parts = lax.axis_size("grp"), lax.axis_size("blk")
    kcount = occupied_offsets.shape[0]
    group = lax.axis_index("grp")

    part = lax.axis_index("blk")
    scalars = (
        jnp.stack([group, part]).astype(jnp.int32),
        tile_owner,
        tile_mask.reshape(-1),
    )

    def swap(values, axis, size, distance):
        return lax.ppermute(values, axis, [(at, at ^ distance) for at in range(size)])

    greens = jnp.stack(
        [
            jnp.swapaxes(occupied_tiles.reshape(-1, tile, tile), 1, 2),
            virtual_tiles.reshape(-1, tile, tile),
        ]
    )
    held = greens.shape[1]
    greens = jnp.stack([greens] + [swap(greens, "grp", planes, j) for j in range(1, planes)])
    near_two = picked_rows(scalars, integrals, 1, (3,))
    across_off = picked_rows(scalars, integrals, 2, (1,))

    slot = jnp.arange(NT, dtype=jnp.int32)
    ordered = jnp.zeros((NT,), jnp.int32).at[tile_owner].set(slot)
    ordered = (ordered // columns ^ group) * columns + ordered % columns
    nearby = (slot // columns ^ group) * columns + slot % columns

    def table(targets, offsets, order):
        natural = (targets[:, None] - offsets[None, :]) % NT
        flat = natural * kcount + jnp.arange(kcount, dtype=jnp.int32)[None, :]
        device = flat // held
        plane, other = device // parts ^ group, device % parts ^ part
        at = ((other * planes + plane) * held) + flat % held
        return order[natural].reshape(-1), at.reshape(-1)

    plane = ordered // columns
    halved = (plane % 2 * 2 + plane // 2) * columns + ordered % columns
    occupied_table = table(tile_owner[nearby], occupied_offsets, ordered)
    virtual_table = table(tile_owner, virtual_offsets, halved)

    greens, near_two, across_off, scalars = lax.optimization_barrier(
        (greens, near_two, across_off, scalars)
    )
    greens = [greens, swap(greens, "blk", parts, 1)] + [
        swap(greens, "blk", parts, m) for m in (2, 4)
    ]
    near_two = swap(near_two, "grp", planes, 1)
    across_off = swap(across_off, "grp", planes, 2)
    near_three = picked_rows(scalars, integrals, 1, (2,))
    across = picked_square(scalars, integrals, 2)
    pairs = list(pair_tiles(scalars, integrals, parts))

    greens, near_two, across_off, near_three, across, pairs, scalars = lax.optimization_barrier(
        (greens, near_two, across_off, near_three, across, pairs, scalars)
    )
    greens = greens[:2] + [
        greens[2],
        swap(greens[2], "blk", parts, 1),
        greens[3],
        swap(greens[3], "blk", parts, 1),
        swap(greens[0], "blk", parts, 6),
    ]
    near_three = swap(near_three, "grp", planes, 1)
    across = swap(across, "grp", planes, 2)
    near = picked_square(scalars, integrals, 1)
    far = picked_square(scalars, integrals, 3)
    own = picked_rows(scalars, integrals, 0, (0, 1, 2, 3))

    greens, near_three, across, near, far, own, pairs, occupied_table, virtual_table = (
        lax.optimization_barrier(
            (greens, near_three, across, near, far, own, pairs, occupied_table, virtual_table)
        )
    )
    greens = greens + [swap(greens[6], "blk", parts, 1)]
    near = swap(near, "grp", planes, 1)
    far = swap(far, "grp", planes, 3)
    for m in (1, 2, 3):
        pairs[m] = swap(pairs[m], "blk", parts, 2 * m)

    where = scalars[0]

    def vmem(*shape, dtype=jnp.bfloat16):
        return pltpu.VMEM(shape, dtype)

    devices = planes * parts
    green = vmem(devices * held, tile, tile)

    def full(count):
        return vmem(basis_size, count * width)

    def half(count):
        return jax.ShapeDtypeStruct((count * columns, basis_size, tile), jnp.bfloat16)

    def folded(offsets):
        return (
            jax.ShapeDtypeStruct(
                (devices, len(offsets), columns, tile // parts, tile), jnp.bfloat16
            ),
            vmem(NT, len(offsets), tile, tile, dtype=jnp.float32),
        )

    column_blocks = (
        tuple((0, plane, False) for plane in range(planes)),
        ((0, 2, True), (1, 0, True), (3, None, False), (2, 0, False)),
    )
    first = kernel_call(
        functools.partial(early_kernel, kcount, column_blocks, len(greens)),
        occupied_table,
        greens,
        (own, near_two, across_off, across),
        half(2),
        [green, full(2), pltpu.SemaphoreType.DMA((devices,))],
        "early_half",
        flops=2 * basis_size * kcount * tile * 2 * width * 2,
    )
    first, near, far = lax.optimization_barrier((first, near, far))
    column_blocks = (
        ((0, 1, True), (4, None, False), (1, 0, False), (2, 0, False)),
        ((0, 3, True), (2, 0, True), (3, 0, True), (5, None, False)),
    )
    out_shape, scratch = folded(CHUNKS[0])
    sent, second = kernel_call(
        functools.partial(last_kernel, kcount, columns, column_blocks, CHUNKS[0], len(greens)),
        (where,) + occupied_table + virtual_table,
        [*greens, first],
        (own, near_two, near_three, across_off, near, far),
        (out_shape, half(2)),
        [
            green,
            green,
            full(2),
            vmem(NT, basis_size, tile),
            scratch,
            pltpu.SemaphoreType.DMA((devices,)),
            pltpu.SemaphoreType.DMA((devices + 1,)),
        ],
        "last_half_and_pairs",
    )
    sent, second, pairs = lax.optimization_barrier((sent, second, pairs))
    pairs[4] = swap(pairs[4], "blk", parts, 7)
    out_shape, scratch = folded(CHUNKS[1])
    rest = kernel_call(
        functools.partial(rest_kernel, kcount, columns, CHUNKS[1], len(greens)),
        (where,) + virtual_table,
        [*greens, first, second],
        (),
        out_shape,
        [
            green,
            vmem(NT, basis_size, tile),
            scratch,
            pltpu.SemaphoreType.DMA((devices + 2,)),
        ],
        "other_pairs",
        flops=2 * 14 * basis_size * kcount * tile * tile * 2,
    )

    def everyone(values):
        return lax.all_to_all(values, ("grp", "blk"), split_axis=0, concat_axis=0, tiled=True)

    sent = everyone(sent)
    sent, rest = lax.optimization_barrier((sent, rest))
    rest = everyone(rest)
    pairs = [
        each
        for mine in pairs[:3]
        for each in (mine[0], swap(mine[1], "blk", parts, 1))
    ] + [pairs[3][0], pairs[4][0]]

    pairs = jnp.stack(pairs)
    partial_sum = 0.0
    at = 0
    for offsets, each in zip(CHUNKS, (sent, rest)):
        theirs = pairs[:, :, at : at + len(offsets)].reshape(parts * aux_local, -1)
        at += len(offsets)
        partial_sum = partial_sum + jnp.einsum(
            "pe,qe->pq", each.reshape(devices, -1), theirs, preferred_element_type=jnp.float32
        )
    partial_sum = partial_sum * (1.0 / basis_size)
    partial_sum = partial_sum.reshape(planes, parts, parts, aux_local)
    partial_sum = partial_sum[:, :, jnp.arange(parts, dtype=jnp.int32) ^ part]
    partial_sum = partial_sum.swapaxes(0, 1).reshape(1, parts, planes, -1)
    spread = jnp.broadcast_to(partial_sum, (planes,) + partial_sum.shape[1:])
    spread = everyone(spread.reshape((devices,) + partial_sum.shape[2:]))
    return jnp.sum(spread, axis=0)


def solution(mesh):
    planes, parts = mesh.shape["grp"], mesh.shape["blk"]

    def body(*args):
        aux_local, basis_size, width = args[0].shape
        tile = basis_size // NT
        fits = aux_local == planes == 4 and parts == 8 and width % tile == 0 and tile % (16 * parts) == 0
        return (folded_body if fits else general_body)(*args)

    in_specs = (
        P("blk", None, "grp"),
        P(),
        P(),
        P(("grp", "blk"), None),
        P(),
        P(("grp", "blk"), None),
        P(),
    )
    out_specs = P("blk", None)
    return jax.shard_map(body, mesh=mesh, in_specs=in_specs, out_specs=out_specs, check_vma=False)
```

```python
import functools

import jax
import jax.numpy as jnp
from jax import lax
from jax.experimental import pallas as pl
from jax.experimental.pallas import tpu as pltpu
from jax.sharding import PartitionSpec as P

NT = 16
CHUNKS = ((0, NT // 2, 1), (2, 3, 4, 5, 6, 7))
OFFSETS = CHUNKS[0] + CHUNKS[1]
PARTS = ((0, 1), (2, 3), (4, 5), (6,), (7,))
UNROLL = 4
VMEM_BYTES = 60 * 1024 * 1024


def general_body(
    integrals,
    tile_mask,
    tile_owner,
    occupied_tiles,
    occupied_offsets,
    virtual_tiles,
    virtual_offsets,
):
    aux_local, basis_size, local_width = integrals.shape
    tile_width = basis_size // NT
    kcount = occupied_offsets.shape[0]
    local_tiles = local_width // tile_width
    group_index = lax.axis_index("grp")
    local_owner = lax.dynamic_slice_in_dim(tile_owner, group_index * local_tiles, local_tiles)
    matches = (local_owner[None, :, None] == jnp.arange(NT, dtype=jnp.int32)[None, None, :]).astype(
        jnp.int32
    )
    column_mask = jnp.sum(tile_mask[:, None, :] * matches, axis=2)
    blocked = integrals.reshape(aux_local, NT, tile_width, local_tiles, tile_width)
    masked = blocked * column_mask.astype(jnp.bfloat16)[None, :, None, :, None]
    masked = masked.reshape(aux_local, NT, tile_width, local_width)
    occupied_all, virtual_all = (
        lax.all_gather(occupied_tiles, ("grp", "blk"), axis=0, tiled=True),
        lax.all_gather(virtual_tiles, ("grp", "blk"), axis=0, tiled=True),
    )
    occupied_all = occupied_all.reshape(NT, kcount, tile_width, tile_width)
    virtual_all = virtual_all.reshape(NT, kcount, tile_width, tile_width)
    source_rows = (tile_owner[:, None] - occupied_offsets[None, :]) % NT
    partner_rows = (tile_owner[:, None] + virtual_offsets[None, :]) % NT
    virtual_pick = virtual_all[tile_owner]
    occupied_sum = jnp.zeros((aux_local, NT, tile_width, local_width), jnp.float32)
    virtual_sum = jnp.zeros((aux_local, local_width, NT, tile_width), jnp.float32)
    for slot in range(kcount):
        occupied_pick = occupied_all[source_rows[:, slot], slot]
        occupied_inputs = masked[:, source_rows[:, slot]]
        occupied_sum = occupied_sum + jnp.einsum(
            "tmn,ptml->ptnl", occupied_pick, occupied_inputs, preferred_element_type=jnp.float32
        )
        virtual_inputs = masked[:, partner_rows[:, slot]]
        virtual_sum = virtual_sum + jnp.einsum(
            "tnm,ptml->pltn",
            virtual_pick[:, slot],
            virtual_inputs,
            preferred_element_type=jnp.float32,
        )
    occupied_part = occupied_sum.astype(jnp.bfloat16)
    virtual_part = virtual_sum.astype(jnp.bfloat16).reshape(
        aux_local, local_tiles, tile_width, basis_size
    )
    occupied_moved = lax.all_to_all(occupied_part, "grp", split_axis=1, concat_axis=3, tiled=True)
    occupied_full, virtual_full = (
        lax.all_to_all(occupied_moved, "blk", split_axis=2, concat_axis=0, tiled=True),
        lax.all_to_all(virtual_part, "blk", split_axis=2, concat_axis=0, tiled=True),
    )
    left_side = occupied_full.reshape(occupied_full.shape[0], -1)
    right_side = virtual_full.reshape(virtual_full.shape[0], -1)
    partial_sum = jnp.einsum(
        "pe,qe->pq", left_side, right_side, preferred_element_type=jnp.float32
    ) * (1.0 / basis_size)
    total = lax.psum(partial_sum, ("grp", "blk"))
    return lax.dynamic_slice_in_dim(total, lax.axis_index("blk") * aux_local, aux_local, 0)


def place(refs, tile_row, column):
    owner_ref, mask_ref = refs
    return mask_ref[tile_row * NT + owner_ref[column]]


def masked_tile(values, kept):
    return values * jnp.full(values.shape, kept, jnp.int32).astype(values.dtype)


def picked_kernel(columns, planes_of, where_ref, owner_ref, mask_ref, *refs):
    inputs, out_ref = refs[:-1], refs[-1]
    tile = out_ref.shape[1]
    group = where_ref[0]
    row_plane = planes_of(pl.program_id(0)) ^ group
    for q in range(columns):
        tile_row = owner_ref[row_plane * columns + q]
        for c in range(columns):
            lanes = slice(c * tile, (c + 1) * tile)
            kept = place((owner_ref, mask_ref), tile_row, group * columns + c)
            out_ref[q, :, lanes] = masked_tile(inputs[q][0, 0, :, lanes], kept)


def triangle(columns):
    return [(q, c) for q in range(columns) for c in range(q + 1)]


def picked_square_kernel(columns, where_ref, owner_ref, mask_ref, *refs):
    inputs, out_ref = refs[:-1], refs[-1]
    tile = out_ref.shape[1]
    first = where_ref[0] * columns
    for at, (q, c) in enumerate(triangle(columns)):
        kept = place((owner_ref, mask_ref), owner_ref[first + q], first + c)
        out_ref[at] = masked_tile(inputs[q][0, 0, :, c * tile : (c + 1) * tile], kept)


def picked_square(scalars, integrals, away):
    aux_local, basis_size, width = integrals.shape
    tile = basis_size // NT
    columns = width // tile
    count = len(triangle(columns))

    def row_map(q):
        def index(i, where, owner, mask):
            return (where[0] ^ away, owner[where[0] * columns + q], 0, 0)

        return index

    return pl.pallas_call(
        functools.partial(picked_square_kernel, columns),
        grid_spec=pltpu.PrefetchScalarGridSpec(
            num_scalar_prefetch=3,
            grid=(1,),
            in_specs=[pl.BlockSpec((1, 1, tile, width), row_map(q)) for q in range(columns)],
            out_specs=pl.BlockSpec((count, tile, tile), lambda i, *_: (0, 0, 0)),
        ),
        out_shape=jax.ShapeDtypeStruct((count, tile, tile), jnp.bfloat16),
        compiler_params=pltpu.CompilerParams(vmem_limit_bytes=VMEM_BYTES),
        cost_estimate=pl.CostEstimate(flops=0, bytes_accessed=0, transcendentals=0),
        name="picked_square",
    )(*scalars, *([integrals.reshape(aux_local, NT, tile, width)] * columns))


def picked_rows(scalars, integrals, away, row_planes):
    aux_local, basis_size, width = integrals.shape
    tile = basis_size // NT
    columns = width // tile

    def planes_of(i):
        return sum(jnp.where(i == at, plane, 0) for at, plane in enumerate(row_planes))

    def row_map(q):
        def index(i, where, owner, mask):
            plane = planes_of(i) ^ where[0]
            return (where[0] ^ away, owner[plane * columns + q], 0, 0)

        return index

    return pl.pallas_call(
        functools.partial(picked_kernel, columns, planes_of),
        grid_spec=pltpu.PrefetchScalarGridSpec(
            num_scalar_prefetch=3,
            grid=(len(row_planes),),
            in_specs=[pl.BlockSpec((1, 1, tile, width), row_map(q)) for q in range(columns)],
            out_specs=pl.BlockSpec((columns, tile, width), lambda i, *_: (i, 0, 0)),
        ),
        out_shape=jax.ShapeDtypeStruct((len(row_planes) * columns, tile, width), jnp.bfloat16),
        compiler_params=pltpu.CompilerParams(vmem_limit_bytes=VMEM_BYTES),
        cost_estimate=pl.CostEstimate(flops=0, bytes_accessed=0, transcendentals=0),
        name="picked_rows",
    )(*scalars, *([integrals.reshape(aux_local, NT, tile, width)] * columns))


def offset_at(i):
    return sum(jnp.where(i == at, offset, 0) for at, offset in enumerate(OFFSETS))


def strips_of(columns, offsets):
    return sum(
        columns * 3 // 4 if d == 0 else columns // 2 if d == NT // 2 else columns for d in offsets
    )


def diagonal_strips(tiles, turned):
    rows, lanes = tiles[0].shape[-2] // 2, tiles[0].shape[-1] // 2
    shape = tiles[0].shape[:-2] + (rows, 2 * lanes)
    left = lax.broadcasted_iota(jnp.int32, shape, len(shape) - 1) < lanes
    kept, rest = [], []
    for c in range(0, len(tiles), 2):
        lower, upper = tiles[c][..., rows:, :], tiles[c + 1][..., :rows, :]
        if turned:
            lower = lower + jnp.where(left, tiles[c].T[rows:, :], 0)
            upper = upper + jnp.where(left, 0, tiles[c + 1].T[:rows, :])
        kept += [lower, upper]
        rest.append(jnp.where(left, tiles[c][..., :rows, :], tiles[c + 1][..., rows:, :]))
    halves = kept + rest
    return [
        jnp.concatenate(halves[at : at + 2], axis=-2) for at in range(0, len(halves), 2)
    ]


def pair_kernel(columns, where_ref, owner_ref, mask_ref, *refs):
    inputs, out_refs, whole = refs[:columns], refs[columns:-1], refs[-1]
    rows, tile = out_refs[0].shape[3:]
    aux_local = out_refs[0].shape[1]
    first = where_ref[0] * columns
    step = pl.program_id(0)

    def tiles():
        for c in range(columns):
            tile_row = owner_ref[lax.rem(first + c + offset_at(step), NT)]
            kept = place((owner_ref, mask_ref), tile_row, first + c)
            yield masked_tile(inputs[c][:, 0], kept)

    def write(strip, values):
        whole[...] = values
        for out_ref, some in zip(out_refs, PARTS):
            for at, part in enumerate(some):
                start = pl.multiple_of((part ^ where_ref[1]) * rows, rows)
                out_ref[at, :, strip] = whole[:, pl.ds(start, rows), :]

    @pl.when(step == 0)
    def _():
        for strip, values in enumerate(diagonal_strips(list(tiles()), False)):
            write(strip, values)

    @pl.when(step == 1)
    def _():
        half = tile // 2
        late = jnp.full((half, tile), first, jnp.int32) >= NT // 2
        halves = []
        for each in tiles():
            halves.append(
                jnp.stack(
                    [
                        jnp.where(late, each[at].T[half:], each[at][:half])
                        for at in range(aux_local)
                    ]
                )
            )
        for at in range(0, columns, 2):
            write(
                strips_of(columns, (0,)) + at // 2,
                jnp.concatenate(halves[at : at + 2], axis=1),
            )

    @pl.when(step > 1)
    def _():
        strip = strips_of(columns, OFFSETS[:2]) + (step - 2) * columns
        for c, values in enumerate(tiles()):
            write(strip + c, values)


def pair_tiles(scalars, integrals, parts):
    aux_local, basis_size, width = integrals.shape
    tile = basis_size // NT
    columns = width // tile
    rows = tile // parts
    shapes = [
        (len(some), aux_local, strips_of(columns, OFFSETS), rows, tile) for some in PARTS
    ]

    def row_map(c):
        def index(d, where, owner, mask):
            return (0, owner[lax.rem(where[0] * columns + c + offset_at(d), NT)], 0, c)

        return index

    return pl.pallas_call(
        functools.partial(pair_kernel, columns),
        grid_spec=pltpu.PrefetchScalarGridSpec(
            num_scalar_prefetch=3,
            grid=(len(OFFSETS),),
            in_specs=[
                pl.BlockSpec((aux_local, 1, tile, tile), row_map(c)) for c in range(columns)
            ],
            out_specs=[pl.BlockSpec(shape, lambda d, *_: (0, 0, 0, 0, 0)) for shape in shapes],
            scratch_shapes=[pltpu.VMEM((aux_local, tile, tile), jnp.bfloat16)],
        ),
        out_shape=[jax.ShapeDtypeStruct(shape, jnp.bfloat16) for shape in shapes],
        compiler_params=pltpu.CompilerParams(vmem_limit_bytes=VMEM_BYTES),
        cost_estimate=pl.CostEstimate(flops=0, bytes_accessed=0, transcendentals=0),
        name="pair_tiles",
    )(*scalars, *([integrals.reshape(aux_local, NT, tile, width)] * columns))


def start_all(copies):
    for copy in copies:
        copy.start()


def wait_all(copies):
    for copy in copies:
        copy.wait()


def green_copies(green_refs, which, green, sems):
    copies = []
    for ref in green_refs:
        held = ref.shape[2]
        for plane in range(ref.shape[0]):
            at = len(copies)
            copies.append(
                pltpu.make_async_copy(
                    ref.at[plane, which], green.at[pl.ds(at * held, held)], sems.at[at]
                )
            )
    return copies


def column_planes(column_blocks, block_refs, tile, full):
    width = full.shape[1] // len(column_blocks)
    columns = width // tile
    for at, blocks in enumerate(column_blocks):
        for plane, (ref, first, turned) in enumerate(blocks):
            if first is None:
                for i, (q, c) in enumerate(triangle(columns)):
                    row, column = plane * width + q * tile, at * width + c * tile
                    values = block_refs[ref][i]
                    full[row : row + tile, column : column + tile] = values
                    if q != c:
                        row, column = plane * width + c * tile, at * width + q * tile
                        full[row : row + tile, column : column + tile] = values.T
                continue
            values = block_refs[ref][first * columns : (first + 1) * columns]
            values = values.reshape(width, width)
            full[plane * width : (plane + 1) * width, at * width : (at + 1) * width] = (
                values.T if turned else values
            )


def occupied_rows(kcount, count, width, slot_ref, tile_ref, green, full, half, first, start, stop):
    tile = green.shape[1]
    columns = width // tile

    @pl.loop(start, stop, unroll=UNROLL)
    def _(r):
        left = jnp.concatenate([green[tile_ref[r * kcount + k]] for k in range(kcount)], axis=1)
        starts = [pl.multiple_of(slot_ref[r * kcount + k] * tile, tile) for k in range(kcount)]
        rows = pl.ds(pl.multiple_of(r * tile, tile), tile)
        for at in range(count):
            right = jnp.concatenate(
                [full[pl.ds(start, tile), at * width : (at + 1) * width] for start in starts],
                axis=0,
            )
            values = jnp.dot(left, right, preferred_element_type=jnp.float32).astype(jnp.bfloat16)
            for c in range(columns):
                half[first + at * columns + c, rows, :] = values[:, c * tile : (c + 1) * tile]


def folded_pairs(kcount, columns, offsets, group, slot_ref, tile_ref, green, half, folded, out_ref):
    tile = green.shape[1]
    pieces = [(at, d, False) for at, d in enumerate(offsets)]
    pieces += [(at, NT - d, True) for at, d in enumerate(offsets) if 0 < d < NT // 2]
    middle = offsets.index(NT // 2) if NT // 2 in offsets else None

    def column(s, late):
        right = jnp.concatenate([green[tile_ref[s * kcount + k]] for k in range(kcount)], axis=0)
        slots = [slot_ref[s * kcount + k] for k in range(kcount)]
        for first in range(0, len(pieces), 4):
            some = pieces[first : first + 4]
            rows = [lax.rem(s + shift, NT) for _, shift, _ in some]
            left = []
            for r in rows:
                start = ((r // columns) ^ group) * columns + lax.rem(r, columns)
                start = pl.multiple_of(start * tile, tile)
                left.append(
                    jnp.concatenate([half[slot, pl.ds(start, tile), :] for slot in slots], axis=1)
                )
            values = jnp.dot(
                jnp.concatenate(left, axis=0), right, preferred_element_type=jnp.float32
            )
            for place_at, ((at, _, turned), r) in enumerate(zip(some, rows)):
                piece = values[place_at * tile : (place_at + 1) * tile]
                if turned or (at == middle and late):
                    folded[r, at] += piece.T
                else:
                    folded[s, at] += piece

    if middle is None:
        pl.loop(0, NT, unroll=UNROLL)(lambda s: column(s, False))
    else:
        pl.loop(0, NT // 2, unroll=UNROLL)(lambda s: column(s, False))
        pl.loop(NT // 2, NT, unroll=UNROLL)(lambda s: column(s, True))

    rows = out_ref.shape[2]
    parts = tile // rows

    @pl.loop(0, NT // columns)
    def _(plane):
        first = plane * columns
        strips = []
        for at, d in enumerate(offsets):
            if d == 0:
                strips += diagonal_strips([folded[first + c, at] for c in range(columns)], True)
            elif d == NT // 2:
                half_rows = pl.ds(
                    pl.multiple_of(first // (NT // 2) * (tile // 2), tile // 2), tile // 2
                )
                halves = [
                    folded[lax.rem(first + c, NT // 2), at, half_rows] for c in range(columns)
                ]
                strips += [
                    jnp.concatenate(halves[c : c + 2], axis=0) for c in range(0, columns, 2)
                ]
            else:
                strips += [folded[first + c, at] for c in range(columns)]
        for strip, values in enumerate(strips):
            values = values.astype(jnp.bfloat16)
            for part in range(parts):
                out_ref[plane * parts + part, strip] = values[part * rows : (part + 1) * rows]


def early_kernel(kcount, column_blocks, parts, slot_ref, tile_ref, *refs):
    green_refs, refs = refs[:parts], refs[parts:]
    block_refs, (out_ref, green, full, half, sems, out_sems) = refs[:-6], refs[-6:]
    width = full.shape[1] // len(column_blocks)
    copies = green_copies(green_refs, 0, green, sems)
    start_all(copies)
    column_planes(column_blocks, block_refs, green.shape[1], full)
    wait_all(copies)
    copies = []
    rows = half.shape[1] // 2
    for at in range(2):
        occupied_rows(
            kcount, len(column_blocks), width, slot_ref, tile_ref, green, full, half, 0,
            at * NT // 2, (at + 1) * NT // 2,
        )
        some = pl.ds(at * rows, rows)
        copies.append(
            pltpu.make_async_copy(half.at[:, some], out_ref.at[:, some], out_sems.at[at])
        )
        copies[-1].start()
    wait_all(copies)


def last_kernel(
    kcount, columns, column_blocks, offsets, parts, group_ref, slot_ref, tile_ref, half_slot_ref,
    virtual_tile_ref, *refs
):
    green_refs, refs = refs[:parts], refs[parts:]
    held_ref, own_ref, refs = refs[0], refs[1], refs[2:]
    block_refs, refs = refs[:-11], refs[-11:]
    (
        out_ref, new_ref, green, virtual, full, half, folded, own, sems, others, own_sems
    ) = refs
    count = held_ref.shape[0]
    width = full.shape[1] // len(column_blocks)
    own_copies = [
        pltpu.make_async_copy(
            own_ref.at[pl.ds((2 * at + 1) * columns, columns)],
            own.at[pl.ds(at * columns, columns)],
            own_sems.at[at],
        )
        for at in range(len(column_blocks))
    ]
    start_all(own_copies)
    copies = green_copies(green_refs, 0, green, sems)
    start_all(copies)
    folded[...] = jnp.zeros_like(folded)
    wait_all(own_copies)
    column_planes(column_blocks, (own, *block_refs), green.shape[1], full)
    wait_all(copies)
    last = others.shape[0] - 1
    later = green_copies(green_refs, 1, virtual, others)
    later.append(
        pltpu.make_async_copy(held_ref, half.at[pl.ds(0, count)], others.at[last - 1])
    )
    start_all(later)
    occupied_rows(
        kcount, len(column_blocks), width, slot_ref, tile_ref, green, full, half, count, 0, NT
    )
    kept = pltpu.make_async_copy(
        half.at[pl.ds(count, new_ref.shape[0])], new_ref, others.at[last]
    )
    kept.start()
    wait_all(later)
    folded_pairs(
        kcount, columns, offsets, group_ref[0], half_slot_ref, virtual_tile_ref, virtual, half,
        folded, out_ref,
    )
    kept.wait()


def rest_kernel(
    kcount, columns, offsets, parts, group_ref, half_slot_ref, virtual_tile_ref, *refs
):
    green_refs, refs = refs[:parts], refs[parts:]
    held_ref, new_ref, out_ref, virtual, half, folded, others = refs
    copies = green_copies(green_refs, 1, virtual, others)
    count = held_ref.shape[0]
    last = others.shape[0] - 1
    copies.append(pltpu.make_async_copy(held_ref, half.at[pl.ds(0, count)], others.at[last - 1]))
    copies.append(
        pltpu.make_async_copy(new_ref, half.at[pl.ds(count, new_ref.shape[0])], others.at[last])
    )
    start_all(copies)
    folded[...] = jnp.zeros_like(folded)
    wait_all(copies)
    folded_pairs(
        kcount, columns, offsets, group_ref[0], half_slot_ref, virtual_tile_ref, virtual, half,
        folded, out_ref,
    )


def kernel_call(
    kernel, tables, anywhere, blocks, out_shape, out_spaces, scratch_shapes, name, flops=0
):
    return pl.pallas_call(
        kernel,
        in_specs=[pl.BlockSpec(memory_space=pltpu.SMEM)] * len(tables)
        + [pl.BlockSpec(memory_space=pl.ANY)] * len(anywhere)
        + [pl.BlockSpec(memory_space=pltpu.VMEM)] * len(blocks),
        out_specs=[pl.BlockSpec(memory_space=space) for space in out_spaces],
        out_shape=out_shape,
        scratch_shapes=scratch_shapes,
        compiler_params=pltpu.CompilerParams(vmem_limit_bytes=VMEM_BYTES),
        cost_estimate=pl.CostEstimate(flops=flops, bytes_accessed=flops // 512, transcendentals=0),
        name=name,
    )(*tables, *anywhere, *blocks)


def folded_body(
    integrals,
    tile_mask,
    tile_owner,
    occupied_tiles,
    occupied_offsets,
    virtual_tiles,
    virtual_offsets,
):
    aux_local, basis_size, width = integrals.shape
    tile = basis_size // NT
    columns = width // tile
    planes, parts = lax.axis_size("grp"), lax.axis_size("blk")
    kcount = occupied_offsets.shape[0]
    group = lax.axis_index("grp")

    part = lax.axis_index("blk")
    scalars = (
        jnp.stack([group, part]).astype(jnp.int32),
        tile_owner,
        tile_mask.reshape(-1),
    )

    def swap(values, axis, size, distance):
        return lax.ppermute(values, axis, [(at, at ^ distance) for at in range(size)])

    greens = jnp.stack(
        [
            jnp.swapaxes(occupied_tiles.reshape(-1, tile, tile), 1, 2),
            virtual_tiles.reshape(-1, tile, tile),
        ]
    )
    held = greens.shape[1]
    greens = jnp.stack([greens] + [swap(greens, "grp", planes, j) for j in range(1, planes)])
    near_two = picked_rows(scalars, integrals, 1, (3,))
    across_off = picked_rows(scalars, integrals, 2, (1,))

    slot = jnp.arange(NT, dtype=jnp.int32)
    ordered = jnp.zeros((NT,), jnp.int32).at[tile_owner].set(slot)
    ordered = (ordered // columns ^ group) * columns + ordered % columns
    nearby = (slot // columns ^ group) * columns + slot % columns

    def table(targets, offsets, order):
        natural = (targets[:, None] - offsets[None, :]) % NT
        flat = natural * kcount + jnp.arange(kcount, dtype=jnp.int32)[None, :]
        device = flat // held
        plane, other = device // parts ^ group, device % parts ^ part
        at = ((other * planes + plane) * held) + flat % held
        return order[natural].reshape(-1), at.reshape(-1)

    plane = ordered // columns
    halved = (plane % 2 * 2 + plane // 2) * columns + ordered % columns
    occupied_table = table(tile_owner[nearby], occupied_offsets, ordered)
    virtual_table = table(tile_owner, virtual_offsets, halved)

    greens, near_two, across_off, scalars = lax.optimization_barrier(
        (greens, near_two, across_off, scalars)
    )
    greens = [greens, swap(greens, "blk", parts, 1)] + [
        swap(greens, "blk", parts, m) for m in (2, 4)
    ]
    near_two = swap(near_two, "grp", planes, 1)
    across_off = swap(across_off, "grp", planes, 2)
    near_three = picked_rows(scalars, integrals, 1, (2,))
    across = picked_square(scalars, integrals, 2)
    pairs = list(pair_tiles(scalars, integrals, parts))

    greens, near_two, across_off, near_three, across, pairs, scalars = lax.optimization_barrier(
        (greens, near_two, across_off, near_three, across, pairs, scalars)
    )
    greens = greens[:2] + [
        greens[2],
        swap(greens[2], "blk", parts, 1),
        greens[3],
        swap(greens[3], "blk", parts, 1),
        swap(greens[0], "blk", parts, 6),
    ]
    near_three = swap(near_three, "grp", planes, 1)
    across = swap(across, "grp", planes, 2)
    near = picked_square(scalars, integrals, 1)
    far = picked_square(scalars, integrals, 3)
    own = picked_rows(scalars, integrals, 0, (0, 1, 2, 3))

    greens, near_three, across, near, far, own, pairs, occupied_table, virtual_table = (
        lax.optimization_barrier(
            (greens, near_three, across, near, far, own, pairs, occupied_table, virtual_table)
        )
    )
    greens = greens + [swap(greens[6], "blk", parts, 1)]
    near = swap(near, "grp", planes, 1)
    far = swap(far, "grp", planes, 3)
    for m in (1, 2, 3):
        pairs[m] = swap(pairs[m], "blk", parts, 2 * m)

    where = scalars[0]

    def vmem(*shape, dtype=jnp.bfloat16):
        return pltpu.VMEM(shape, dtype)

    devices = planes * parts
    green = vmem(devices * held, tile, tile)

    def full(count):
        return vmem(basis_size, count * width)

    def half(count):
        return jax.ShapeDtypeStruct((count * columns, basis_size, tile), jnp.bfloat16)

    def folded(offsets):
        return (
            jax.ShapeDtypeStruct(
                (devices, strips_of(columns, offsets), tile // parts, tile), jnp.bfloat16
            ),
            vmem(NT, len(offsets), tile, tile, dtype=jnp.float32),
        )

    column_blocks = (
        tuple((0, plane, False) for plane in range(planes)),
        ((0, 2, True), (1, 0, True), (3, None, False), (2, 0, False)),
    )
    (first,) = kernel_call(
        functools.partial(early_kernel, kcount, column_blocks, len(greens)),
        occupied_table,
        greens,
        (own, near_two, across_off, across),
        [half(2)],
        [pl.ANY],
        [
            green,
            full(2),
            vmem(2 * columns, basis_size, tile),
            pltpu.SemaphoreType.DMA((devices,)),
            pltpu.SemaphoreType.DMA((2,)),
        ],
        "early_half",
        flops=2 * basis_size * kcount * tile * 2 * width * 2,
    )
    first, near, far = lax.optimization_barrier((first, near, far))
    column_blocks = (
        ((0, 0, True), (4, None, False), (1, 0, False), (2, 0, False)),
        ((0, 1, True), (2, 0, True), (3, 0, True), (5, None, False)),
    )
    out_shape, scratch = folded(CHUNKS[0])
    sent, second = kernel_call(
        functools.partial(last_kernel, kcount, columns, column_blocks, CHUNKS[0], len(greens)),
        (where,) + occupied_table + virtual_table,
        [*greens, first, own],
        (near_two, near_three, across_off, near, far),
        [out_shape, half(2)],
        [pltpu.VMEM, pl.ANY],
        [
            green,
            green,
            full(2),
            vmem(NT, basis_size, tile),
            scratch,
            vmem(2 * columns, tile, width),
            pltpu.SemaphoreType.DMA((devices,)),
            pltpu.SemaphoreType.DMA((devices + 2,)),
            pltpu.SemaphoreType.DMA((2,)),
        ],
        "last_half_and_pairs",
    )
    sent, second, pairs[:3], pairs[4] = lax.optimization_barrier(
        (sent, second, pairs[:3], pairs[4])
    )
    pairs[4] = swap(pairs[4], "blk", parts, 7)
    out_shape, scratch = folded(CHUNKS[1])
    (rest,) = kernel_call(
        functools.partial(rest_kernel, kcount, columns, CHUNKS[1], len(greens)),
        (where,) + virtual_table,
        [*greens, first, second],
        (),
        [out_shape],
        [pltpu.VMEM],
        [
            green,
            vmem(NT, basis_size, tile),
            scratch,
            pltpu.SemaphoreType.DMA((devices + 2,)),
        ],
        "other_pairs",
        flops=2 * 12 * basis_size * kcount * tile * tile * 2,
    )

    def everyone(values):
        return lax.all_to_all(values, ("grp", "blk"), split_axis=0, concat_axis=0, tiled=True)

    sent = everyone(sent)
    sent, rest, pairs[3] = lax.optimization_barrier((sent, rest, pairs[3]))
    rest = everyone(rest)
    pairs = [
        each
        for mine in pairs[:3]
        for each in (mine[0], swap(mine[1], "blk", parts, 1))
    ] + [pairs[3][0], pairs[4][0]]

    pairs = jnp.stack(pairs)
    partial_sum = 0.0
    at = 0
    for offsets, each in zip(CHUNKS, (sent, rest)):
        count = strips_of(columns, offsets)
        theirs = pairs[:, :, at : at + count].reshape(parts * aux_local, -1)
        at += count
        partial_sum = partial_sum + jnp.einsum(
            "pe,qe->pq", each.reshape(devices, -1), theirs, preferred_element_type=jnp.float32
        )
    partial_sum = partial_sum * (1.0 / basis_size)
    partial_sum = partial_sum.reshape(planes, parts, parts, aux_local)
    partial_sum = partial_sum[:, :, jnp.arange(parts, dtype=jnp.int32) ^ part]
    partial_sum = partial_sum.swapaxes(0, 1).reshape(1, parts, planes, -1)
    spread = jnp.broadcast_to(partial_sum, (planes,) + partial_sum.shape[1:])
    spread = everyone(spread.reshape((devices,) + partial_sum.shape[2:]))
    return jnp.sum(spread, axis=0)


def solution(mesh):
    planes, parts = mesh.shape["grp"], mesh.shape["blk"]

    def body(*args):
        aux_local, basis_size, width = args[0].shape
        tile = basis_size // NT
        fits = aux_local == planes == 4 and parts == 8 and width % tile == 0 and tile % (16 * parts) == 0 and width == 4 * tile
        return (folded_body if fits else general_body)(*args)

    in_specs = (
        P("blk", None, "grp"),
        P(),
        P(),
        P(("grp", "blk"), None),
        P(),
        P(("grp", "blk"), None),
        P(),
    )
    out_specs = P("blk", None)
    return jax.shard_map(body, mesh=mesh, in_specs=in_specs, out_specs=out_specs, check_vma=False)
```

```python
import functools

import jax
import jax.numpy as jnp
from jax import lax
from jax.experimental import pallas as pl
from jax.experimental.pallas import tpu as pltpu
from jax.sharding import PartitionSpec as P

NT = 16
UNROLL = 4
VMEM_BYTES = 60 * 1024 * 1024
PARTS = (
    ((0, 0), (0, 1), (1, 0), (1, 1)),
    ((2, 0), (2, 1), (3, 0), (3, 1)),
    ((4, 0), (4, 1), (5, 0), (5, 1)),
    ((7, 0), (7, 1), (6, 0)),
    ((6, 1),),
)


def general_body(
    integrals,
    tile_mask,
    tile_owner,
    occupied_tiles,
    occupied_offsets,
    virtual_tiles,
    virtual_offsets,
):
    aux_local, basis_size, local_width = integrals.shape
    tile_width = basis_size // NT
    kcount = occupied_offsets.shape[0]
    local_tiles = local_width // tile_width
    group_index = lax.axis_index("grp")
    local_owner = lax.dynamic_slice_in_dim(tile_owner, group_index * local_tiles, local_tiles)
    matches = (local_owner[None, :, None] == jnp.arange(NT, dtype=jnp.int32)[None, None, :]).astype(
        jnp.int32
    )
    column_mask = jnp.sum(tile_mask[:, None, :] * matches, axis=2)
    blocked = integrals.reshape(aux_local, NT, tile_width, local_tiles, tile_width)
    masked = blocked * column_mask.astype(jnp.bfloat16)[None, :, None, :, None]
    masked = masked.reshape(aux_local, NT, tile_width, local_width)
    occupied_all, virtual_all = (
        lax.all_gather(occupied_tiles, ("grp", "blk"), axis=0, tiled=True),
        lax.all_gather(virtual_tiles, ("grp", "blk"), axis=0, tiled=True),
    )
    occupied_all = occupied_all.reshape(NT, kcount, tile_width, tile_width)
    virtual_all = virtual_all.reshape(NT, kcount, tile_width, tile_width)
    source_rows = (tile_owner[:, None] - occupied_offsets[None, :]) % NT
    partner_rows = (tile_owner[:, None] + virtual_offsets[None, :]) % NT
    virtual_pick = virtual_all[tile_owner]
    occupied_sum = jnp.zeros((aux_local, NT, tile_width, local_width), jnp.float32)
    virtual_sum = jnp.zeros((aux_local, local_width, NT, tile_width), jnp.float32)
    for slot in range(kcount):
        occupied_pick = occupied_all[source_rows[:, slot], slot]
        occupied_inputs = masked[:, source_rows[:, slot]]
        occupied_sum = occupied_sum + jnp.einsum(
            "tmn,ptml->ptnl", occupied_pick, occupied_inputs, preferred_element_type=jnp.float32
        )
        virtual_inputs = masked[:, partner_rows[:, slot]]
        virtual_sum = virtual_sum + jnp.einsum(
            "tnm,ptml->pltn",
            virtual_pick[:, slot],
            virtual_inputs,
            preferred_element_type=jnp.float32,
        )
    occupied_part = occupied_sum.astype(jnp.bfloat16)
    virtual_part = virtual_sum.astype(jnp.bfloat16).reshape(
        aux_local, local_tiles, tile_width, basis_size
    )
    occupied_moved = lax.all_to_all(occupied_part, "grp", split_axis=1, concat_axis=3, tiled=True)
    occupied_full, virtual_full = (
        lax.all_to_all(occupied_moved, "blk", split_axis=2, concat_axis=0, tiled=True),
        lax.all_to_all(virtual_part, "blk", split_axis=2, concat_axis=0, tiled=True),
    )
    left_side = occupied_full.reshape(occupied_full.shape[0], -1)
    right_side = virtual_full.reshape(virtual_full.shape[0], -1)
    partial_sum = jnp.einsum(
        "pe,qe->pq", left_side, right_side, preferred_element_type=jnp.float32
    ) * (1.0 / basis_size)
    total = lax.psum(partial_sum, ("grp", "blk"))
    return lax.dynamic_slice_in_dim(total, lax.axis_index("blk") * aux_local, aux_local, 0)


def place(refs, tile_row, column):
    owner_ref, mask_ref = refs
    return mask_ref[tile_row * NT + owner_ref[column]]


def masked_tile(values, kept):
    return values * jnp.full(values.shape, kept, jnp.int32).astype(values.dtype)


def picked_kernel(columns, planes_of, where_ref, owner_ref, mask_ref, *refs):
    inputs, out_ref = refs[:-1], refs[-1]
    tile = out_ref.shape[1]
    group = where_ref[0]
    row_plane = planes_of(pl.program_id(0)) ^ group
    for q in range(columns):
        tile_row = owner_ref[row_plane * columns + q]
        for c in range(columns):
            lanes = slice(c * tile, (c + 1) * tile)
            kept = place((owner_ref, mask_ref), tile_row, group * columns + c)
            out_ref[q, :, lanes] = masked_tile(inputs[q][0, 0, :, lanes], kept)


def triangle(columns):
    return [(q, c) for q in range(columns) for c in range(q + 1)]


def picked_square_kernel(columns, planes, where_ref, owner_ref, mask_ref, *refs):
    inputs, out_ref = refs[:-1], refs[-1]
    tile = out_ref.shape[1]
    first = where_ref[0] * columns
    wanted = [(0, q, c) for q, c in triangle(columns)]
    wanted += [(i, q, c) for i in range(1, len(planes)) for q in range(columns) for c in range(columns)]
    for at, (i, q, c) in enumerate(wanted):
        row = owner_ref[(where_ref[0] ^ planes[i]) * columns + q]
        kept = place((owner_ref, mask_ref), row, first + c)
        out_ref[at] = masked_tile(inputs[i * columns + q][0, 0, :, c * tile : (c + 1) * tile], kept)


def picked_square(scalars, integrals, away, planes=(0,)):
    aux_local, basis_size, width = integrals.shape
    tile = basis_size // NT
    columns = width // tile
    count = len(triangle(columns)) + (len(planes) - 1) * columns * columns

    def row_map(plane, q):
        def index(i, where, owner, mask):
            return (where[0] ^ away, owner[(where[0] ^ plane) * columns + q], 0, 0)

        return index

    return pl.pallas_call(
        functools.partial(picked_square_kernel, columns, planes),
        grid_spec=pltpu.PrefetchScalarGridSpec(
            num_scalar_prefetch=3,
            grid=(1,),
            in_specs=[
                pl.BlockSpec((1, 1, tile, width), row_map(plane, q))
                for plane in planes
                for q in range(columns)
            ],
            out_specs=pl.BlockSpec((count, tile, tile), lambda i, *_: (0, 0, 0)),
        ),
        out_shape=jax.ShapeDtypeStruct((count, tile, tile), jnp.bfloat16),
        compiler_params=pltpu.CompilerParams(vmem_limit_bytes=VMEM_BYTES),
        cost_estimate=pl.CostEstimate(flops=0, bytes_accessed=0, transcendentals=0),
        name="picked_square",
    )(*scalars, *([integrals.reshape(aux_local, NT, tile, width)] * (columns * len(planes))))


def picked_rows(scalars, integrals, away, row_planes):
    aux_local, basis_size, width = integrals.shape
    tile = basis_size // NT
    columns = width // tile

    def planes_of(i):
        return sum(jnp.where(i == at, plane, 0) for at, plane in enumerate(row_planes))

    def row_map(q):
        def index(i, where, owner, mask):
            plane = planes_of(i) ^ where[0]
            return (where[0] ^ away, owner[plane * columns + q], 0, 0)

        return index

    return pl.pallas_call(
        functools.partial(picked_kernel, columns, planes_of),
        grid_spec=pltpu.PrefetchScalarGridSpec(
            num_scalar_prefetch=3,
            grid=(len(row_planes),),
            in_specs=[pl.BlockSpec((1, 1, tile, width), row_map(q)) for q in range(columns)],
            out_specs=pl.BlockSpec((columns, tile, width), lambda i, *_: (i, 0, 0)),
        ),
        out_shape=jax.ShapeDtypeStruct((len(row_planes) * columns, tile, width), jnp.bfloat16),
        compiler_params=pltpu.CompilerParams(vmem_limit_bytes=VMEM_BYTES),
        cost_estimate=pl.CostEstimate(flops=0, bytes_accessed=0, transcendentals=0),
        name="picked_rows",
    )(*scalars, *([integrals.reshape(aux_local, NT, tile, width)] * columns))


def strips_of(columns):
    square = columns * columns
    return 2 * square, columns * 3 // 4 + (square - columns) // 2 + square // 2


def diagonal_strips(tiles, turned):
    rows, lanes = tiles[0].shape[-2] // 2, tiles[0].shape[-1] // 2
    shape = tiles[0].shape[:-2] + (rows, 2 * lanes)
    left = lax.broadcasted_iota(jnp.int32, shape, len(shape) - 1) < lanes
    kept, rest = [], []
    for c in range(0, len(tiles), 2):
        lower, upper = tiles[c][..., rows:, :], tiles[c + 1][..., :rows, :]
        if turned:
            lower = lower + jnp.where(left, tiles[c].T[rows:, :], 0)
            upper = upper + jnp.where(left, 0, tiles[c + 1].T[:rows, :])
        kept += [lower, upper]
        rest.append(jnp.where(left, tiles[c][..., :rows, :], tiles[c + 1][..., rows:, :]))
    halves = kept + rest
    return [
        jnp.concatenate(halves[at : at + 2], axis=-2) for at in range(0, len(halves), 2)
    ]


def pair_kernel(columns, where_ref, owner_ref, mask_ref, *refs):
    inputs, out_refs, (whole,) = refs[:columns], refs[columns:-1], refs[-1:]
    rows, tile = out_refs[0].shape[3:]
    first = where_ref[0] * columns
    step = pl.program_id(0)
    plane = where_ref[0] ^ pair_plane(step)
    cross, _ = strips_of(columns)
    within = cross + columns * 3 // 4
    sibling = within + (columns * columns - columns) // 2
    starts = [
        [(pl.multiple_of((part ^ where_ref[1]) * rows, rows), at) for part, at in some]
        for some in PARTS
    ]

    def masked(q, c):
        kept = place((owner_ref, mask_ref), owner_ref[plane * columns + q], first + c)
        return masked_tile(inputs[q][:, 0, :, c * tile : (c + 1) * tile], kept)

    def write(strip, strips):
        for at, values in enumerate(strips):
            whole[at] = values
        for out_ref, some in zip(out_refs, starts):
            count = out_ref.shape[1]
            for piece, (start, aux) in enumerate(some):
                for at in range(len(strips)):
                    out_ref[piece, :, strip + at] = whole[
                        at, aux * count : (aux + 1) * count, pl.ds(start, rows), :
                    ]

    @pl.when(step < 2)
    def _():
        for q in range(columns):
            write((step * columns + q) * columns, [masked(q, c) for c in range(columns)])

    @pl.when(step == 2)
    def _():
        write(cross, diagonal_strips([masked(c, c) for c in range(columns)], False))
        write(within, [masked(q, c) for q in range(columns) for c in range(q)])

    @pl.when((step == 3) & (where_ref[0] % 2 == 0))
    def _():
        write(sibling, [masked(q, c) for q in range(columns // 2) for c in range(columns)])

    @pl.when((step == 3) & (where_ref[0] % 2 == 1))
    def _():
        write(
            sibling, [masked(q, c) for q in range(columns) for c in range(columns // 2, columns)]
        )


def pair_plane(k):
    return jnp.where(k < 2, k + 2, k - 2)


def pair_tiles(scalars, integrals, parts):
    aux_local, basis_size, width = integrals.shape
    tile = basis_size // NT
    columns = width // tile
    rows = tile // parts
    shapes = [
        (len(some), aux_local // 2, sum(strips_of(columns)), rows, tile) for some in PARTS
    ]

    def row_map(q):
        def index(i, where, owner, mask):
            return (0, owner[(where[0] ^ pair_plane(i)) * columns + q], 0, 0)

        return index

    return pl.pallas_call(
        functools.partial(pair_kernel, columns),
        grid_spec=pltpu.PrefetchScalarGridSpec(
            num_scalar_prefetch=3,
            grid=(NT // columns,),
            in_specs=[
                pl.BlockSpec((aux_local, 1, tile, width), row_map(q)) for q in range(columns)
            ],
            out_specs=[pl.BlockSpec(shape, lambda i, *_: (0, 0, 0, 0, 0)) for shape in shapes],
            scratch_shapes=[
                pltpu.VMEM((columns * columns // 2, aux_local, tile, tile), jnp.bfloat16)
            ],
        ),
        out_shape=[jax.ShapeDtypeStruct(shape, jnp.bfloat16) for shape in shapes],
        compiler_params=pltpu.CompilerParams(vmem_limit_bytes=VMEM_BYTES),
        cost_estimate=pl.CostEstimate(flops=0, bytes_accessed=0, transcendentals=0),
        name="pair_tiles",
    )(*scalars, *([integrals.reshape(aux_local, NT, tile, width)] * columns))


def start_all(copies):
    for copy in copies:
        copy.start()


def wait_all(copies):
    for copy in copies:
        copy.wait()


def green_copies(green_refs, which, green, sems):
    copies = []
    for ref in green_refs:
        held = ref.shape[2]
        for plane in range(ref.shape[0]):
            at = len(copies)
            copies.append(
                pltpu.make_async_copy(
                    ref.at[plane, which], green.at[pl.ds(at * held, held)], sems.at[at]
                )
            )
    return copies


def column_planes(column_blocks, block_refs, tile, full):
    width = full.shape[1] // len(column_blocks)
    columns = width // tile
    for at, blocks in enumerate(column_blocks):
        for plane, (ref, first, turned) in enumerate(blocks):
            if first is None:
                for i, (q, c) in enumerate(triangle(columns)):
                    row, column = plane * width + q * tile, at * width + c * tile
                    values = block_refs[ref][i]
                    full[row : row + tile, column : column + tile] = values
                    if q != c:
                        row, column = plane * width + c * tile, at * width + q * tile
                        full[row : row + tile, column : column + tile] = values.T
                continue
            if block_refs[ref].shape[2] == tile:
                count = len(triangle(columns)) + (first - 1) * columns * columns
                for i in range(columns * columns):
                    q, c = i // columns, i % columns
                    if turned:
                        q, c = c, q
                    row, column = plane * width + q * tile, at * width + c * tile
                    values = block_refs[ref][count + i]
                    full[row : row + tile, column : column + tile] = values.T if turned else values
                continue
            values = block_refs[ref][first * columns : (first + 1) * columns]
            values = values.reshape(width, width)
            full[plane * width : (plane + 1) * width, at * width : (at + 1) * width] = (
                values.T if turned else values
            )


def occupied_rows(kcount, count, width, slot_ref, tile_ref, green, full, half, first, start, stop):
    tile = green.shape[1]
    columns = width // tile

    @pl.loop(start, stop, unroll=UNROLL)
    def _(r):
        left = jnp.concatenate([green[tile_ref[r * kcount + k]] for k in range(kcount)], axis=1)
        starts = [pl.multiple_of(slot_ref[r * kcount + k] * tile, tile) for k in range(kcount)]
        rows = pl.ds(pl.multiple_of(r * tile, tile), tile)
        for at in range(count):
            right = jnp.concatenate(
                [full[pl.ds(start, tile), at * width : (at + 1) * width] for start in starts],
                axis=0,
            )
            values = jnp.dot(left, right, preferred_element_type=jnp.float32).astype(jnp.bfloat16)
            for c in range(columns):
                half[first + at * columns + c, rows, :] = values[:, c * tile : (c + 1) * tile]


def half_products(kcount, other, slot_ref, tile_ref, green, half, product):
    tile = green.shape[1]
    count = NT // 2

    def column(t, rows):
        right = jnp.concatenate([green[tile_ref[t * kcount + k]] for k in range(kcount)], axis=0)
        slots = [slot_ref[t * kcount + k] for k in range(kcount)]
        for first in range(0, count, 4):
            start = (rows + first) * tile
            left = jnp.concatenate(
                [half[slot, start : start + 4 * tile, :] for slot in slots], axis=1
            )
            values = jnp.dot(left, right, preferred_element_type=jnp.float32)
            product[t, first : first + 4] = values.reshape(4, tile, tile)

    pl.loop(0, count, unroll=UNROLL)(lambda t: column(t, count if other else 0))
    pl.loop(count, NT, unroll=UNROLL)(lambda t: column(t, 0 if other else count))


def write_strip(out_ref, device, strip, values):
    rows = out_ref.shape[2]
    values = values.astype(jnp.bfloat16)
    for part in range(values.shape[0] // rows):
        out_ref[device + part, strip] = values[part * rows : (part + 1) * rows]


def cross_strips(columns, group, product, out_ref):
    count = NT // 2
    parts = out_ref.shape[0] // 2

    @pl.loop(0, 2)
    def _(plane):
        away = plane ^ lax.rem(group, 2)

        @pl.loop(0, 2)
        def _(k):
            first = (k ^ away) * columns
            for q in range(columns):
                for c in range(columns):
                    s = away * columns + c
                    values = product[s, first + q] + product[count + first + q, s].T
                    write_strip(out_ref, plane * parts, (k * columns + q) * columns + c, values)


def within_strips(columns, group, product, out_ref):
    planes = NT // columns
    parts = out_ref.shape[0] // planes

    for plane in range(planes):
        away = plane ^ group
        own, near = lax.rem(away, 2) * columns, (1 - lax.rem(away, 2)) * columns
        first, sibling = away * columns, (away ^ 1) * columns
        tiles = [product[first + c, own + c] for c in range(columns)]
        strips = diagonal_strips(tiles, True)
        for q in range(columns):
            for c in range(q):
                strips.append(product[first + c, own + q] + product[first + q, own + c].T)
        for at in range(columns * columns // 2):
            if plane % 2:
                q, c = at // (columns // 2), columns // 2 + at % (columns // 2)
            else:
                q, c = at // columns, at % columns
            strips.append(product[first + c, near + q] + product[sibling + q, own + c].T)
        for strip, values in enumerate(strips):
            write_strip(out_ref, plane * parts, strip, values)


def first_kernel(
    kcount, columns, column_blocks, parts, group_ref, slot_ref, tile_ref, half_slot_ref,
    virtual_tile_ref, *refs
):
    green_refs, refs = refs[:parts], refs[parts:]
    block_refs, refs = refs[:-9], refs[-9:]
    out_ref, half_ref, green, virtual, full, half, product, sems, others = refs
    width = full.shape[1] // len(column_blocks)
    copies = green_copies(green_refs, 0, green, sems)
    start_all(copies)
    column_planes(column_blocks, block_refs, green.shape[1], full)
    wait_all(copies)
    later = green_copies(green_refs, 1, virtual, others)
    start_all(later)
    occupied_rows(
        kcount, len(column_blocks), width, slot_ref, tile_ref, green, full, half, 0, 0, NT
    )
    kept = pltpu.make_async_copy(half, half_ref, others.at[others.shape[0] - 1])
    kept.start()
    wait_all(later)
    half_products(kcount, False, half_slot_ref, virtual_tile_ref, virtual, half, product)
    within_strips(columns, group_ref[0], product, out_ref)
    kept.wait()


def rest_kernel(
    kcount, columns, parts, group_ref, half_slot_ref, virtual_tile_ref, *refs
):
    green_refs, refs = refs[:parts], refs[parts:]
    half_ref, out_ref, virtual, half, product, others = refs
    copies = green_copies(green_refs, 1, virtual, others)
    copies.append(pltpu.make_async_copy(half_ref, half, others.at[others.shape[0] - 1]))
    start_all(copies)
    wait_all(copies)
    half_products(kcount, True, half_slot_ref, virtual_tile_ref, virtual, half, product)
    cross_strips(columns, group_ref[0], product, out_ref)


def kernel_call(
    kernel, tables, anywhere, blocks, out_shape, out_spaces, scratch_shapes, name, flops=0
):
    return pl.pallas_call(
        kernel,
        in_specs=[pl.BlockSpec(memory_space=pltpu.SMEM)] * len(tables)
        + [pl.BlockSpec(memory_space=pl.ANY)] * len(anywhere)
        + [pl.BlockSpec(memory_space=pltpu.VMEM)] * len(blocks),
        out_specs=[pl.BlockSpec(memory_space=space) for space in out_spaces],
        out_shape=out_shape,
        scratch_shapes=scratch_shapes,
        compiler_params=pltpu.CompilerParams(vmem_limit_bytes=VMEM_BYTES),
        cost_estimate=pl.CostEstimate(flops=flops, bytes_accessed=flops // 512, transcendentals=0),
        name=name,
    )(*tables, *anywhere, *blocks)


def paired_kernel(first, parts, left_ref, *refs):
    right_refs, (out_ref, right, sems) = refs[:parts], refs[parts:]
    sources, count, rows, tile = left_ref.shape
    copies = []
    others = 0
    for at, ref in enumerate(right_refs):
        copies.append(
            pltpu.make_async_copy(
                ref.at[:, pl.ds(first, count)],
                right.at[pl.ds(others, ref.shape[0])],
                sems.at[at],
            )
        )
        others += ref.shape[0]
    start_all(copies)
    wait_all(copies)
    left = jnp.concatenate(
        [left_ref[:, at].reshape(sources * rows, tile) for at in range(count)], axis=1
    )
    right = jnp.concatenate(
        [right[:, at].reshape(others * rows, tile) for at in range(count)], axis=1
    )
    total = lax.dot_general(
        left, right, (((1,), (1,)), ((), ())), preferred_element_type=jnp.float32
    )
    down = lax.broadcasted_iota(jnp.int32, total.shape, 0)
    along = lax.broadcasted_iota(jnp.int32, total.shape, 1)
    total = jnp.where((down ^ along) % rows == 0, total, 0.0)
    total = jnp.sum(total.reshape(sources, rows, others * rows), axis=1)
    out_ref[...] = jnp.sum(total.T.reshape(others, rows, sources), axis=1)


def paired(left, rights, first, count):
    parts = len(rights)
    others = sum(each.shape[0] for each in rights)
    return pl.pallas_call(
        functools.partial(paired_kernel, first, parts),
        in_specs=[pl.BlockSpec(memory_space=pltpu.VMEM)]
        + [pl.BlockSpec(memory_space=pl.ANY)] * parts,
        out_specs=pl.BlockSpec(memory_space=pltpu.VMEM),
        out_shape=jax.ShapeDtypeStruct((others, left.shape[0]), jnp.float32),
        scratch_shapes=[
            pltpu.VMEM((others, count) + left.shape[2:], jnp.bfloat16),
            pltpu.SemaphoreType.DMA((parts,)),
        ],
        compiler_params=pltpu.CompilerParams(vmem_limit_bytes=VMEM_BYTES),
        name="paired",
    )(left, *rights)


def folded_body(
    integrals,
    tile_mask,
    tile_owner,
    occupied_tiles,
    occupied_offsets,
    virtual_tiles,
    virtual_offsets,
):
    aux_local, basis_size, width = integrals.shape
    tile = basis_size // NT
    columns = width // tile
    planes, parts = lax.axis_size("grp"), lax.axis_size("blk")
    kcount = occupied_offsets.shape[0]
    group = lax.axis_index("grp")

    part = lax.axis_index("blk")
    scalars = (
        jnp.stack([group, part]).astype(jnp.int32),
        tile_owner,
        tile_mask.reshape(-1),
    )

    def swap(values, axis, size, distance):
        return lax.ppermute(values, axis, [(at, at ^ distance) for at in range(size)])

    greens = jnp.stack(
        [
            jnp.swapaxes(occupied_tiles.reshape(-1, tile, tile), 1, 2),
            virtual_tiles.reshape(-1, tile, tile),
        ]
    )
    held = greens.shape[1]
    greens = jnp.stack([greens] + [swap(greens, "grp", planes, j) for j in range(1, planes)])
    pairs = list(pair_tiles(scalars, integrals, parts))
    pairs[3] = swap(pairs[3], "blk", parts, 6)
    near_off = picked_rows(scalars, integrals, 1, (3, 2))
    across = picked_square(scalars, integrals, 2, (0, 1))

    slot = jnp.arange(NT, dtype=jnp.int32)
    ordered = jnp.zeros((NT,), jnp.int32).at[tile_owner].set(slot)
    ordered = (ordered // columns ^ group) * columns + ordered % columns
    nearby = (slot // columns ^ group) * columns + slot % columns

    def table(targets, offsets):
        natural = (targets[:, None] - offsets[None, :]) % NT
        flat = natural * kcount + jnp.arange(kcount, dtype=jnp.int32)[None, :]
        device = flat // held
        plane, other = device // parts ^ group, device % parts ^ part
        at = ((other * planes + plane) * held) + flat % held
        return ordered[natural].reshape(-1), at.reshape(-1)

    occupied_table = table(tile_owner[nearby], occupied_offsets)
    virtual_table = table(tile_owner[nearby], virtual_offsets)

    greens, near_off, across, scalars = lax.optimization_barrier(
        (greens, near_off, across, scalars)
    )
    greens = [greens] + [swap(greens, "blk", parts, m) for m in (2, 4)]
    near_off = swap(near_off, "grp", planes, 1)
    across = swap(across, "grp", planes, 2)
    near = picked_square(scalars, integrals, 1)
    far = picked_square(scalars, integrals, 3)

    greens, near_off, across, near, far, pairs, scalars = lax.optimization_barrier(
        (greens, near_off, across, near, far, pairs, scalars)
    )
    greens = [
        greens[0],
        greens[1],
        swap(greens[1], "blk", parts, 1),
        greens[2],
        swap(greens[1][: planes // 2], "blk", parts, 4),
        swap(greens[2][planes // 2 :], "blk", parts, 2),
    ]
    near = swap(near, "grp", planes, 1)
    far = swap(far, "grp", planes, 3)
    own = picked_rows(scalars, integrals, 0, (0, 1, 2, 3))

    greens, near, far, own, pairs, occupied_table, virtual_table = lax.optimization_barrier(
        (greens, near, far, own, pairs, occupied_table, virtual_table)
    )
    greens = [
        greens[0],
        swap(greens[0], "blk", parts, 1),
        *greens[1:4],
        swap(greens[3], "blk", parts, 1),
        *greens[4:],
        swap(greens[4], "blk", parts, 1),
        swap(greens[5], "blk", parts, 1),
    ]
    for m in (1, 2):
        pairs[m] = swap(pairs[m], "blk", parts, 2 * m)

    where = scalars[0]

    def vmem(*shape, dtype=jnp.bfloat16):
        return pltpu.VMEM(shape, dtype)

    devices = planes * parts
    green = vmem(devices * held, tile, tile)

    cross, within = strips_of(columns)

    def strips(count, strips):
        return jax.ShapeDtypeStruct((count, strips, tile // parts, tile), jnp.bfloat16)

    product = vmem(NT, NT // 2, tile, tile, dtype=jnp.float32)

    column_blocks = (
        ((0, 0, False), (0, 1, False), (0, 2, False), (0, 3, False)),
        ((0, 1, True), (1, None, False), (2, 0, False), (2, 1, False)),
        ((0, 2, True), (2, 0, True), (3, None, False), (3, 1, False)),
        ((0, 3, True), (2, 1, True), (3, 1, True), (4, None, False)),
    )
    half = vmem(NT, basis_size, tile)
    sent, halves = kernel_call(
        functools.partial(first_kernel, kcount, columns, column_blocks, len(greens)),
        (where,) + occupied_table + virtual_table,
        greens,
        (own, near, near_off, across, far),
        [strips(devices, within), jax.ShapeDtypeStruct((NT, basis_size, tile), jnp.bfloat16)],
        [pltpu.VMEM, pl.ANY],
        [
            green,
            green,
            vmem(basis_size, basis_size),
            half,
            product,
            pltpu.SemaphoreType.DMA((devices,)),
            pltpu.SemaphoreType.DMA((devices + 1,)),
        ],
        "half_and_pairs",
    )
    sent, halves, pairs = lax.optimization_barrier((sent, halves, pairs))
    pairs[4] = swap(pairs[4], "blk", parts, 6)
    pairs[3:] = [pairs[3][2:], pairs[4], swap(pairs[3][:2], "blk", parts, 1)]
    pairs = [
        each
        for mine in pairs[:3]
        for each in (mine[:2], swap(mine[2:], "blk", parts, 1))
    ] + pairs[3:]
    (rest,) = kernel_call(
        functools.partial(rest_kernel, kcount, columns, len(greens)),
        (where,) + virtual_table,
        [*greens, halves],
        (),
        [strips(2 * parts, cross)],
        [pltpu.VMEM],
        [
            green,
            half,
            product,
            pltpu.SemaphoreType.DMA((devices + 1,)),
        ],
        "other_pairs",
        flops=2 * 8 * basis_size * kcount * tile * tile * 2,
    )

    def everyone(values, groups=None):
        return lax.all_to_all(
            values, ("grp", "blk"), split_axis=0, concat_axis=0, tiled=True,
            axis_index_groups=groups,
        )

    sent = everyone(sent)
    sent, rest, pairs = lax.optimization_barrier((sent, rest, pairs))
    rest = everyone(rest, [list(range(2 * parts)), list(range(2 * parts, devices))])
    pairs = [each.reshape((-1,) + each.shape[2:]) for each in pairs]

    partial_sum = paired(sent, pairs, cross, within).reshape(-1, 2, 2, parts)
    here = (jnp.arange(2, dtype=jnp.int32) == group // 2)[:, None, None]
    crossing = paired(rest, pairs, 0, cross).reshape(-1, 1, 2, parts)
    partial_sum = (partial_sum + jnp.where(here, crossing, 0.0)) * (1.0 / basis_size)
    partial_sum = partial_sum.reshape(parts, aux_local, planes, parts)
    partial_sum = partial_sum[jnp.arange(parts, dtype=jnp.int32) ^ part]
    partial_sum = partial_sum.transpose(3, 2, 0, 1).reshape(1, parts, planes, -1)
    spread = jnp.broadcast_to(partial_sum, (planes,) + partial_sum.shape[1:])
    spread = everyone(spread.reshape((devices,) + partial_sum.shape[2:]))
    return jnp.sum(spread, axis=0)


def solution(mesh):
    planes, parts = mesh.shape["grp"], mesh.shape["blk"]

    def body(*args):
        aux_local, basis_size, width = args[0].shape
        tile = basis_size // NT
        fits = aux_local == planes == 4 and parts == 8 and width % tile == 0 and tile % (16 * parts) == 0 and width == 4 * tile
        return (folded_body if fits else general_body)(*args)

    in_specs = (
        P("blk", None, "grp"),
        P(),
        P(),
        P(("grp", "blk"), None),
        P(),
        P(("grp", "blk"), None),
        P(),
    )
    out_specs = P("blk", None)
    return jax.shard_map(body, mesh=mesh, in_specs=in_specs, out_specs=out_specs, check_vma=False)
```

```python
import functools

import jax
import jax.numpy as jnp
from jax import lax
from jax.experimental import pallas as pl
from jax.experimental.pallas import tpu as pltpu
from jax.sharding import PartitionSpec as P

NT = 16
UNROLL = 4
STEPS = 2
VMEM_BYTES = 60 * 1024 * 1024
PARTS = (
    ((0, 0), (0, 1), (1, 0), (1, 1)),
    ((2, 0), (2, 1), (3, 0), (3, 1)),
    ((4, 0), (4, 1), (5, 0), (5, 1)),
    ((7, 0), (7, 1), (6, 0)),
    ((6, 1),),
)


def general_body(
    integrals,
    tile_mask,
    tile_owner,
    occupied_tiles,
    occupied_offsets,
    virtual_tiles,
    virtual_offsets,
):
    aux_local, basis_size, local_width = integrals.shape
    tile_width = basis_size // NT
    kcount = occupied_offsets.shape[0]
    local_tiles = local_width // tile_width
    group_index = lax.axis_index("grp")
    local_owner = lax.dynamic_slice_in_dim(tile_owner, group_index * local_tiles, local_tiles)
    matches = (local_owner[None, :, None] == jnp.arange(NT, dtype=jnp.int32)[None, None, :]).astype(
        jnp.int32
    )
    column_mask = jnp.sum(tile_mask[:, None, :] * matches, axis=2)
    blocked = integrals.reshape(aux_local, NT, tile_width, local_tiles, tile_width)
    masked = blocked * column_mask.astype(jnp.bfloat16)[None, :, None, :, None]
    masked = masked.reshape(aux_local, NT, tile_width, local_width)
    occupied_all, virtual_all = (
        lax.all_gather(occupied_tiles, ("grp", "blk"), axis=0, tiled=True),
        lax.all_gather(virtual_tiles, ("grp", "blk"), axis=0, tiled=True),
    )
    occupied_all = occupied_all.reshape(NT, kcount, tile_width, tile_width)
    virtual_all = virtual_all.reshape(NT, kcount, tile_width, tile_width)
    source_rows = (tile_owner[:, None] - occupied_offsets[None, :]) % NT
    partner_rows = (tile_owner[:, None] + virtual_offsets[None, :]) % NT
    virtual_pick = virtual_all[tile_owner]
    occupied_sum = jnp.zeros((aux_local, NT, tile_width, local_width), jnp.float32)
    virtual_sum = jnp.zeros((aux_local, local_width, NT, tile_width), jnp.float32)
    for slot in range(kcount):
        occupied_pick = occupied_all[source_rows[:, slot], slot]
        occupied_inputs = masked[:, source_rows[:, slot]]
        occupied_sum = occupied_sum + jnp.einsum(
            "tmn,ptml->ptnl", occupied_pick, occupied_inputs, preferred_element_type=jnp.float32
        )
        virtual_inputs = masked[:, partner_rows[:, slot]]
        virtual_sum = virtual_sum + jnp.einsum(
            "tnm,ptml->pltn",
            virtual_pick[:, slot],
            virtual_inputs,
            preferred_element_type=jnp.float32,
        )
    occupied_part = occupied_sum.astype(jnp.bfloat16)
    virtual_part = virtual_sum.astype(jnp.bfloat16).reshape(
        aux_local, local_tiles, tile_width, basis_size
    )
    occupied_moved = lax.all_to_all(occupied_part, "grp", split_axis=1, concat_axis=3, tiled=True)
    occupied_full, virtual_full = (
        lax.all_to_all(occupied_moved, "blk", split_axis=2, concat_axis=0, tiled=True),
        lax.all_to_all(virtual_part, "blk", split_axis=2, concat_axis=0, tiled=True),
    )
    left_side = occupied_full.reshape(occupied_full.shape[0], -1)
    right_side = virtual_full.reshape(virtual_full.shape[0], -1)
    partial_sum = jnp.einsum(
        "pe,qe->pq", left_side, right_side, preferred_element_type=jnp.float32
    ) * (1.0 / basis_size)
    total = lax.psum(partial_sum, ("grp", "blk"))
    return lax.dynamic_slice_in_dim(total, lax.axis_index("blk") * aux_local, aux_local, 0)


def place(refs, tile_row, column):
    owner_ref, mask_ref = refs
    return mask_ref[tile_row * NT + owner_ref[column]]


def masked_tile(values, kept):
    return values * jnp.full(values.shape, kept, jnp.int32).astype(values.dtype)


def picked_kernel(columns, planes_of, where_ref, owner_ref, mask_ref, *refs):
    inputs, out_ref = refs[:-1], refs[-1]
    tile = out_ref.shape[1]
    group = where_ref[0]
    row_plane = planes_of(pl.program_id(0)) ^ group
    for q in range(columns):
        tile_row = owner_ref[row_plane * columns + q]
        for c in range(columns):
            lanes = slice(c * tile, (c + 1) * tile)
            kept = place((owner_ref, mask_ref), tile_row, group * columns + c)
            out_ref[q, :, lanes] = masked_tile(inputs[q][0, 0, :, lanes], kept)


def triangle(columns):
    return [(q, c) for q in range(columns) for c in range(q + 1)]


def picked_square_kernel(columns, planes, where_ref, owner_ref, mask_ref, *refs):
    inputs, out_ref = refs[:-1], refs[-1]
    tile = out_ref.shape[1]
    first = where_ref[0] * columns
    wanted = [(0, q, c) for q, c in triangle(columns)]
    wanted += [(i, q, c) for i in range(1, len(planes)) for q in range(columns) for c in range(columns)]
    for at, (i, q, c) in enumerate(wanted):
        row = owner_ref[(where_ref[0] ^ planes[i]) * columns + q]
        kept = place((owner_ref, mask_ref), row, first + c)
        out_ref[at] = masked_tile(inputs[i * columns + q][0, 0, :, c * tile : (c + 1) * tile], kept)


def picked_square(scalars, integrals, away, planes=(0,)):
    aux_local, basis_size, width = integrals.shape
    tile = basis_size // NT
    columns = width // tile
    count = len(triangle(columns)) + (len(planes) - 1) * columns * columns

    def row_map(plane, q):
        def index(i, where, owner, mask):
            return (where[0] ^ away, owner[(where[0] ^ plane) * columns + q], 0, 0)

        return index

    return pl.pallas_call(
        functools.partial(picked_square_kernel, columns, planes),
        grid_spec=pltpu.PrefetchScalarGridSpec(
            num_scalar_prefetch=3,
            grid=(1,),
            in_specs=[
                pl.BlockSpec((1, 1, tile, width), row_map(plane, q))
                for plane in planes
                for q in range(columns)
            ],
            out_specs=pl.BlockSpec((count, tile, tile), lambda i, *_: (0, 0, 0)),
        ),
        out_shape=jax.ShapeDtypeStruct((count, tile, tile), jnp.bfloat16),
        compiler_params=pltpu.CompilerParams(vmem_limit_bytes=VMEM_BYTES),
        cost_estimate=pl.CostEstimate(flops=0, bytes_accessed=0, transcendentals=0),
        name="picked_square",
    )(*scalars, *([integrals.reshape(aux_local, NT, tile, width)] * (columns * len(planes))))


def picked_rows(scalars, integrals, away, row_planes):
    aux_local, basis_size, width = integrals.shape
    tile = basis_size // NT
    columns = width // tile

    def planes_of(i):
        return sum(jnp.where(i == at, plane, 0) for at, plane in enumerate(row_planes))

    def row_map(q):
        def index(i, where, owner, mask):
            plane = planes_of(i) ^ where[0]
            return (where[0] ^ away, owner[plane * columns + q], 0, 0)

        return index

    return pl.pallas_call(
        functools.partial(picked_kernel, columns, planes_of),
        grid_spec=pltpu.PrefetchScalarGridSpec(
            num_scalar_prefetch=3,
            grid=(len(row_planes),),
            in_specs=[pl.BlockSpec((1, 1, tile, width), row_map(q)) for q in range(columns)],
            out_specs=pl.BlockSpec((columns, tile, width), lambda i, *_: (i, 0, 0)),
        ),
        out_shape=jax.ShapeDtypeStruct((len(row_planes) * columns, tile, width), jnp.bfloat16),
        compiler_params=pltpu.CompilerParams(vmem_limit_bytes=VMEM_BYTES),
        cost_estimate=pl.CostEstimate(flops=0, bytes_accessed=0, transcendentals=0),
        name="picked_rows",
    )(*scalars, *([integrals.reshape(aux_local, NT, tile, width)] * columns))


def strips_of(columns):
    square = columns * columns
    return 2 * square, columns * 3 // 4 + (square - columns) // 2 + square // 2


def diagonal_strips(tiles, turned):
    rows, lanes = tiles[0].shape[-2] // 2, tiles[0].shape[-1] // 2
    shape = tiles[0].shape[:-2] + (rows, 2 * lanes)
    left = lax.broadcasted_iota(jnp.int32, shape, len(shape) - 1) < lanes
    kept, rest = [], []
    for c in range(0, len(tiles), 2):
        lower, upper = tiles[c][..., rows:, :], tiles[c + 1][..., :rows, :]
        if turned:
            lower = lower + jnp.where(left, tiles[c].T[rows:, :], 0)
            upper = upper + jnp.where(left, 0, tiles[c + 1].T[:rows, :])
        kept += [lower, upper]
        rest.append(jnp.where(left, tiles[c][..., :rows, :], tiles[c + 1][..., rows:, :]))
    halves = kept + rest
    return [
        jnp.concatenate(halves[at : at + 2], axis=-2) for at in range(0, len(halves), 2)
    ]


def pair_kernel(columns, where_ref, owner_ref, mask_ref, *refs):
    inputs, out_refs, (whole,) = refs[:columns], refs[columns:-1], refs[-1:]
    rows, tile = out_refs[0].shape[3:]
    first = where_ref[0] * columns
    step = pl.program_id(0)
    plane = where_ref[0] ^ pair_plane(step)
    cross, _ = strips_of(columns)
    within = cross + columns * 3 // 4
    sibling = within + (columns * columns - columns) // 2
    starts = [
        [(pl.multiple_of((part ^ where_ref[1]) * rows, rows), at) for part, at in some]
        for some in PARTS
    ]

    def masked(q, c):
        kept = place((owner_ref, mask_ref), owner_ref[plane * columns + q], first + c)
        return masked_tile(inputs[q][:, 0, :, c * tile : (c + 1) * tile], kept)

    def write(strip, strips):
        for at, values in enumerate(strips):
            whole[at] = values
        for out_ref, some in zip(out_refs, starts):
            count = out_ref.shape[1]
            for piece, (start, aux) in enumerate(some):
                for at in range(len(strips)):
                    out_ref[piece, :, strip + at] = whole[
                        at, aux * count : (aux + 1) * count, pl.ds(start, rows), :
                    ]

    @pl.when(step < 2)
    def _():
        for q in range(columns):
            write((step * columns + q) * columns, [masked(q, c) for c in range(columns)])

    @pl.when(step == 2)
    def _():
        write(cross, diagonal_strips([masked(c, c) for c in range(columns)], False))
        write(within, [masked(q, c) for q in range(columns) for c in range(q)])

    @pl.when((step == 3) & (where_ref[0] % 2 == 0))
    def _():
        write(sibling, [masked(q, c) for q in range(columns // 2) for c in range(columns)])

    @pl.when((step == 3) & (where_ref[0] % 2 == 1))
    def _():
        write(
            sibling, [masked(q, c) for q in range(columns) for c in range(columns // 2, columns)]
        )


def pair_plane(k):
    return jnp.where(k < 2, k + 2, k - 2)


def pair_tiles(scalars, integrals, parts):
    aux_local, basis_size, width = integrals.shape
    tile = basis_size // NT
    columns = width // tile
    rows = tile // parts
    shapes = [
        (len(some), aux_local // 2, sum(strips_of(columns)), rows, tile) for some in PARTS
    ]

    def row_map(q):
        def index(i, where, owner, mask):
            return (0, owner[(where[0] ^ pair_plane(i)) * columns + q], 0, 0)

        return index

    return pl.pallas_call(
        functools.partial(pair_kernel, columns),
        grid_spec=pltpu.PrefetchScalarGridSpec(
            num_scalar_prefetch=3,
            grid=(NT // columns,),
            in_specs=[
                pl.BlockSpec((aux_local, 1, tile, width), row_map(q)) for q in range(columns)
            ],
            out_specs=[pl.BlockSpec(shape, lambda i, *_: (0, 0, 0, 0, 0)) for shape in shapes],
            scratch_shapes=[
                pltpu.VMEM((columns * columns // 2, aux_local, tile, tile), jnp.bfloat16)
            ],
        ),
        out_shape=[jax.ShapeDtypeStruct(shape, jnp.bfloat16) for shape in shapes],
        compiler_params=pltpu.CompilerParams(vmem_limit_bytes=VMEM_BYTES),
        cost_estimate=pl.CostEstimate(flops=0, bytes_accessed=0, transcendentals=0),
        name="pair_tiles",
    )(*scalars, *([integrals.reshape(aux_local, NT, tile, width)] * columns))


def start_all(copies):
    for copy in copies:
        copy.start()


def wait_all(copies):
    for copy in copies:
        copy.wait()


def green_copies(green_refs, which, green, sems):
    copies = []
    for ref in green_refs:
        held = ref.shape[2]
        for plane in range(ref.shape[0]):
            at = len(copies)
            copies.append(
                pltpu.make_async_copy(
                    ref.at[plane, which], green.at[pl.ds(at * held, held)], sems.at[at]
                )
            )
    return copies


def column_planes(column_blocks, block_refs, tile, full):
    width = full.shape[1] // len(column_blocks)
    columns = width // tile
    for at, blocks in enumerate(column_blocks):
        for plane, (ref, first, turned) in enumerate(blocks):
            if first is None:
                for i, (q, c) in enumerate(triangle(columns)):
                    row, column = plane * width + q * tile, at * width + c * tile
                    values = block_refs[ref][i]
                    full[row : row + tile, column : column + tile] = values
                    if q != c:
                        row, column = plane * width + c * tile, at * width + q * tile
                        full[row : row + tile, column : column + tile] = values.T
                continue
            if block_refs[ref].shape[2] == tile:
                count = len(triangle(columns)) + (first - 1) * columns * columns
                for i in range(columns * columns):
                    q, c = i // columns, i % columns
                    if turned:
                        q, c = c, q
                    row, column = plane * width + q * tile, at * width + c * tile
                    values = block_refs[ref][count + i]
                    full[row : row + tile, column : column + tile] = values.T if turned else values
                continue
            values = block_refs[ref][first * columns : (first + 1) * columns]
            values = values.reshape(width, width)
            full[plane * width : (plane + 1) * width, at * width : (at + 1) * width] = (
                values.T if turned else values
            )


def occupied_rows(kcount, count, width, slot_ref, tile_ref, green, full, half, first, start, stop):
    tile = green.shape[1]
    columns = width // tile

    @pl.loop(start, stop, unroll=UNROLL)
    def _(r):
        left = jnp.concatenate([green[tile_ref[r * kcount + k]] for k in range(kcount)], axis=1)
        starts = [pl.multiple_of(slot_ref[r * kcount + k] * tile, tile) for k in range(kcount)]
        rows = pl.ds(pl.multiple_of(r * tile, tile), tile)
        for at in range(count):
            right = jnp.concatenate(
                [full[pl.ds(start, tile), at * width : (at + 1) * width] for start in starts],
                axis=0,
            )
            values = jnp.dot(left, right, preferred_element_type=jnp.float32).astype(jnp.bfloat16)
            for c in range(columns):
                half[first + at * columns + c, rows, :] = values[:, c * tile : (c + 1) * tile]


def half_products(kcount, other, slot_ref, tile_ref, green, half, product):
    tile = green.shape[1]
    count = NT // 2

    def column(t, rows):
        right = jnp.concatenate([green[tile_ref[t * kcount + k]] for k in range(kcount)], axis=0)
        slots = [slot_ref[t * kcount + k] for k in range(kcount)]
        for first in range(0, count, 4):
            start = (rows + first) * tile
            left = jnp.concatenate(
                [half[slot, start : start + 4 * tile, :] for slot in slots], axis=1
            )
            values = jnp.dot(left, right, preferred_element_type=jnp.float32)
            product[t, first : first + 4] = values.reshape(4, tile, tile)

    pl.loop(0, count, unroll=UNROLL)(lambda t: column(t, count if other else 0))
    pl.loop(count, NT, unroll=UNROLL)(lambda t: column(t, 0 if other else count))


def write_strip(out_ref, device, strip, values):
    rows = out_ref.shape[2]
    values = values.astype(jnp.bfloat16)
    for part in range(values.shape[0] // rows):
        out_ref[device + part, strip] = values[part * rows : (part + 1) * rows]


def cross_strips(columns, group, product, out_ref):
    count = NT // 2
    parts = out_ref.shape[0] // 2

    @pl.loop(0, 2)
    def _(plane):
        away = plane ^ lax.rem(group, 2)

        @pl.loop(0, 2)
        def _(k):
            first = (k ^ away) * columns
            for q in range(columns):
                for c in range(columns):
                    s = away * columns + c
                    values = product[s, first + q] + product[count + first + q, s].T
                    write_strip(out_ref, plane * parts, (k * columns + q) * columns + c, values)


def within_strips(columns, group, product, out_ref):
    planes = NT // columns
    parts = out_ref.shape[0] // planes

    for plane in range(planes):
        away = plane ^ group
        own, near = lax.rem(away, 2) * columns, (1 - lax.rem(away, 2)) * columns
        first, sibling = away * columns, (away ^ 1) * columns
        tiles = [product[first + c, own + c] for c in range(columns)]
        strips = diagonal_strips(tiles, True)
        for q in range(columns):
            for c in range(q):
                strips.append(product[first + c, own + q] + product[first + q, own + c].T)
        for at in range(columns * columns // 2):
            if plane % 2:
                q, c = at // (columns // 2), columns // 2 + at % (columns // 2)
            else:
                q, c = at // columns, at % columns
            strips.append(product[first + c, near + q] + product[sibling + q, own + c].T)
        for strip, values in enumerate(strips):
            write_strip(out_ref, plane * parts, strip, values)


def first_kernel(
    kcount, columns, column_blocks, parts, group_ref, slot_ref, tile_ref, half_slot_ref,
    virtual_tile_ref, *refs
):
    green_refs, refs = refs[:parts], refs[parts:]
    block_refs, refs = refs[:-9], refs[-9:]
    out_ref, half_ref, green, virtual, full, half, product, sems, others = refs
    width = full.shape[1] // len(column_blocks)
    copies = green_copies(green_refs, 0, green, sems)
    start_all(copies)
    column_planes(column_blocks, block_refs, green.shape[1], full)
    wait_all(copies)
    later = green_copies(green_refs, 1, virtual, others)
    start_all(later)
    occupied_rows(
        kcount, len(column_blocks), width, slot_ref, tile_ref, green, full, half, 0, 0, NT
    )
    kept = pltpu.make_async_copy(half, half_ref, others.at[others.shape[0] - 1])
    kept.start()
    wait_all(later)
    half_products(kcount, False, half_slot_ref, virtual_tile_ref, virtual, half, product)
    within_strips(columns, group_ref[0], product, out_ref)
    kept.wait()


def rest_kernel(
    kcount, columns, parts, group_ref, half_slot_ref, virtual_tile_ref, *refs
):
    green_refs, refs = refs[:parts], refs[parts:]
    half_ref, out_ref, virtual, half, product, others = refs
    copies = green_copies(green_refs, 1, virtual, others)
    copies.append(pltpu.make_async_copy(half_ref, half, others.at[others.shape[0] - 1]))
    start_all(copies)
    wait_all(copies)
    half_products(kcount, True, half_slot_ref, virtual_tile_ref, virtual, half, product)
    cross_strips(columns, group_ref[0], product, out_ref)


def kernel_call(
    kernel, tables, anywhere, blocks, out_shape, out_spaces, scratch_shapes, name, flops=0
):
    return pl.pallas_call(
        kernel,
        in_specs=[pl.BlockSpec(memory_space=pltpu.SMEM)] * len(tables)
        + [pl.BlockSpec(memory_space=pl.ANY)] * len(anywhere)
        + [pl.BlockSpec(memory_space=pltpu.VMEM)] * len(blocks),
        out_specs=[pl.BlockSpec(memory_space=space) for space in out_spaces],
        out_shape=out_shape,
        scratch_shapes=scratch_shapes,
        compiler_params=pltpu.CompilerParams(vmem_limit_bytes=VMEM_BYTES),
        cost_estimate=pl.CostEstimate(flops=flops, bytes_accessed=flops // 512, transcendentals=0),
        name=name,
    )(*tables, *anywhere, *blocks)


def paired_kernel(first, steps, parts, columns, where_ref, left_ref, *refs):
    right_refs, refs = refs[:parts], refs[parts:]
    base_refs, (out_ref, left, right, total, sums, sems) = refs[:-6], refs[-6:]
    sources, count, rows, tile = left_ref.shape
    others = right.shape[0]
    some = count // steps
    copies = []
    for step in range(steps):
        here = pl.ds(step * some, some)
        there = pl.ds(first + step * some, some)
        pairs = [(left_ref.at[:, here], left.at[:, here])]
        at = 0
        for ref in right_refs:
            place_at = (at // 4 ^ where_ref[1]) * 4 + at % 4
            pairs.append((ref.at[:, there], right.at[pl.ds(place_at, ref.shape[0]), here]))
            at += ref.shape[0]
        copies.append(
            [
                pltpu.make_async_copy(source, target, sems.at[step * (parts + 1) + i])
                for i, (source, target) in enumerate(pairs)
            ]
        )
    for each in copies:
        start_all(each)
    for step, each in enumerate(copies):
        wait_all(each)
        strips = range(step * some, (step + 1) * some)
        values = lax.dot_general(
            jnp.concatenate([left[:, i].reshape(sources * rows, tile) for i in strips], axis=1),
            jnp.concatenate([right[:, i].reshape(others * rows, tile) for i in strips], axis=1),
            (((1,), (1,)), ((), ())),
            preferred_element_type=jnp.float32,
        )
        if step:
            total[...] += values
        else:
            total[...] = values
    values = total[...]
    down = lax.broadcasted_iota(jnp.int32, values.shape, 0)
    along = lax.broadcasted_iota(jnp.int32, values.shape, 1)
    values = jnp.where((down ^ along) % rows == 0, values, 0.0)
    values = jnp.sum(values.reshape(sources, rows, others * rows), axis=1)
    values = jnp.sum(values.T.reshape(others, rows, sources), axis=1).T
    if not base_refs:
        out_ref[...] = values
        return
    devices = out_ref.shape[0]
    each = devices // columns
    start = pl.multiple_of(where_ref[0] // 2 * sources, sources)
    out_ref[...] = jnp.zeros_like(out_ref)
    sums[...] = base_refs[0][...]
    sums[pl.ds(start, sources), :] += values
    for blk in range(each):
        values = sums[pl.ds(blk, columns, stride=each), :] * (1.0 / (NT * tile))
        for plane in range(columns):
            out_ref[plane * each + blk, :columns, :others] = values


def paired(where, left, rights, first, steps, base=None):
    parts = len(rights)
    sources, count, rows, tile = left.shape
    others = sum(each.shape[0] for each in rights)
    vmem = pl.BlockSpec(memory_space=pltpu.VMEM)
    base = () if base is None else (base,)
    shape = (base[0].shape[0], 8, 128) if base else (sources, others)
    return pl.pallas_call(
        functools.partial(paired_kernel, first, steps, parts, 4),
        in_specs=[pl.BlockSpec(memory_space=pltpu.SMEM)]
        + [pl.BlockSpec(memory_space=pl.ANY)] * (parts + 1)
        + [vmem] * len(base),
        out_specs=vmem,
        out_shape=jax.ShapeDtypeStruct(shape, jnp.float32),
        scratch_shapes=[
            pltpu.VMEM(left.shape, jnp.bfloat16),
            pltpu.VMEM((others,) + left.shape[1:], jnp.bfloat16),
            pltpu.VMEM((sources * rows, others * rows), jnp.float32),
            pltpu.VMEM((others, others), jnp.float32),
            pltpu.SemaphoreType.DMA((steps * (parts + 1),)),
        ],
        compiler_params=pltpu.CompilerParams(vmem_limit_bytes=VMEM_BYTES),
        name="paired",
    )(where, left, *rights, *base)


def folded_body(
    integrals,
    tile_mask,
    tile_owner,
    occupied_tiles,
    occupied_offsets,
    virtual_tiles,
    virtual_offsets,
):
    aux_local, basis_size, width = integrals.shape
    tile = basis_size // NT
    columns = width // tile
    planes, parts = lax.axis_size("grp"), lax.axis_size("blk")
    kcount = occupied_offsets.shape[0]
    group = lax.axis_index("grp")

    part = lax.axis_index("blk")
    scalars = (
        jnp.stack([group, part]).astype(jnp.int32),
        tile_owner,
        tile_mask.reshape(-1),
    )

    def swap(values, axis, size, distance):
        return lax.ppermute(values, axis, [(at, at ^ distance) for at in range(size)])

    greens = jnp.stack(
        [
            jnp.swapaxes(occupied_tiles.reshape(-1, tile, tile), 1, 2),
            virtual_tiles.reshape(-1, tile, tile),
        ]
    )
    held = greens.shape[1]
    greens = jnp.stack([greens] + [swap(greens, "grp", planes, j) for j in range(1, planes)])
    pairs = list(pair_tiles(scalars, integrals, parts))
    pairs[3] = swap(pairs[3], "blk", parts, 6)
    near_off = picked_rows(scalars, integrals, 1, (3, 2))
    across = picked_square(scalars, integrals, 2, (0, 1))

    slot = jnp.arange(NT, dtype=jnp.int32)
    ordered = jnp.zeros((NT,), jnp.int32).at[tile_owner].set(slot)
    ordered = (ordered // columns ^ group) * columns + ordered % columns
    nearby = (slot // columns ^ group) * columns + slot % columns

    def table(targets, offsets):
        natural = (targets[:, None] - offsets[None, :]) % NT
        flat = natural * kcount + jnp.arange(kcount, dtype=jnp.int32)[None, :]
        device = flat // held
        plane, other = device // parts ^ group, device % parts ^ part
        at = ((other * planes + plane) * held) + flat % held
        return ordered[natural].reshape(-1), at.reshape(-1)

    occupied_table = table(tile_owner[nearby], occupied_offsets)
    virtual_table = table(tile_owner[nearby], virtual_offsets)

    greens, near_off, across, scalars = lax.optimization_barrier(
        (greens, near_off, across, scalars)
    )
    greens = [greens] + [swap(greens, "blk", parts, m) for m in (2, 4)]
    near_off = swap(near_off, "grp", planes, 1)
    across = swap(across, "grp", planes, 2)
    near = picked_square(scalars, integrals, 1)
    far = picked_square(scalars, integrals, 3)

    greens, near_off, across, near, far, pairs, scalars = lax.optimization_barrier(
        (greens, near_off, across, near, far, pairs, scalars)
    )
    greens = [
        greens[0],
        greens[1],
        swap(greens[1], "blk", parts, 1),
        greens[2],
        swap(greens[1][: planes // 2], "blk", parts, 4),
        swap(greens[2][planes // 2 :], "blk", parts, 2),
    ]
    near = swap(near, "grp", planes, 1)
    far = swap(far, "grp", planes, 3)
    own = picked_rows(scalars, integrals, 0, (0, 1, 2, 3))

    greens, near, far, own, pairs, occupied_table, virtual_table = lax.optimization_barrier(
        (greens, near, far, own, pairs, occupied_table, virtual_table)
    )
    greens = [
        greens[0],
        swap(greens[0], "blk", parts, 1),
        *greens[1:4],
        swap(greens[3], "blk", parts, 1),
        *greens[4:],
        swap(greens[4], "blk", parts, 1),
        swap(greens[5], "blk", parts, 1),
    ]
    for m in (1, 2):
        pairs[m] = swap(pairs[m], "blk", parts, 2 * m)

    where = scalars[0]

    def vmem(*shape, dtype=jnp.bfloat16):
        return pltpu.VMEM(shape, dtype)

    devices = planes * parts
    green = vmem(devices * held, tile, tile)

    cross, within = strips_of(columns)

    def strips(count, strips):
        return jax.ShapeDtypeStruct((count, strips, tile // parts, tile), jnp.bfloat16)

    product = vmem(NT, NT // 2, tile, tile, dtype=jnp.float32)

    column_blocks = (
        ((0, 0, False), (0, 1, False), (0, 2, False), (0, 3, False)),
        ((0, 1, True), (1, None, False), (2, 0, False), (2, 1, False)),
        ((0, 2, True), (2, 0, True), (3, None, False), (3, 1, False)),
        ((0, 3, True), (2, 1, True), (3, 1, True), (4, None, False)),
    )
    half = vmem(NT, basis_size, tile)
    sent, halves = kernel_call(
        functools.partial(first_kernel, kcount, columns, column_blocks, len(greens)),
        (where,) + occupied_table + virtual_table,
        greens,
        (own, near, near_off, across, far),
        [strips(devices, within), jax.ShapeDtypeStruct((NT, basis_size, tile), jnp.bfloat16)],
        [pltpu.VMEM, pl.ANY],
        [
            green,
            green,
            vmem(basis_size, basis_size),
            half,
            product,
            pltpu.SemaphoreType.DMA((devices,)),
            pltpu.SemaphoreType.DMA((devices + 1,)),
        ],
        "half_and_pairs",
    )
    sent, halves, pairs = lax.optimization_barrier((sent, halves, pairs))
    pairs[4] = swap(pairs[4], "blk", parts, 6)
    pairs[3:] = [pairs[3][2:], pairs[4], swap(pairs[3][:2], "blk", parts, 1)]
    pairs = [
        each
        for mine in pairs[:3]
        for each in (mine[:2], swap(mine[2:], "blk", parts, 1))
    ] + pairs[3:]
    (rest,) = kernel_call(
        functools.partial(rest_kernel, kcount, columns, len(greens)),
        (where,) + virtual_table,
        [*greens, halves],
        (),
        [strips(2 * parts, cross)],
        [pltpu.VMEM],
        [
            green,
            half,
            product,
            pltpu.SemaphoreType.DMA((devices + 1,)),
        ],
        "other_pairs",
        flops=2 * 8 * basis_size * kcount * tile * tile * 2,
    )

    def everyone(values, groups=None):
        return lax.all_to_all(
            values, ("grp", "blk"), split_axis=0, concat_axis=0, tiled=True,
            axis_index_groups=groups,
        )

    sent = everyone(sent)
    sent, rest, pairs = lax.optimization_barrier((sent, rest, pairs))
    rest = everyone(rest, [list(range(2 * parts)), list(range(2 * parts, devices))])
    pairs = [each.reshape((-1,) + each.shape[2:]) for each in pairs]

    total = paired(where, sent, pairs, cross, 1)
    total = jnp.sum(everyone(paired(where, rest, pairs, 0, STEPS, total)), axis=0)
    return total[:aux_local, : parts * aux_local]


def solution(mesh):
    planes, parts = mesh.shape["grp"], mesh.shape["blk"]

    def body(*args):
        aux_local, basis_size, width = args[0].shape
        tile = basis_size // NT
        fits = aux_local == planes == 4 and parts == 8 and width % tile == 0 and tile % (16 * parts) == 0 and width == 4 * tile
        return (folded_body if fits else general_body)(*args)

    in_specs = (
        P("blk", None, "grp"),
        P(),
        P(),
        P(("grp", "blk"), None),
        P(),
        P(("grp", "blk"), None),
        P(),
    )
    out_specs = P("blk", None)
    return jax.shard_map(body, mesh=mesh, in_specs=in_specs, out_specs=out_specs, check_vma=False)
```

```python
import functools

import jax
import jax.numpy as jnp
from jax import lax
from jax.experimental import pallas as pl
from jax.experimental.pallas import tpu as pltpu
from jax.sharding import PartitionSpec as P

NT = 16
UNROLL = 4
PAIRED_BYTES = 24 * 1024 * 1024
VMEM_BYTES = 60 * 1024 * 1024
PARTS = (
    ((0, 0), (0, 1), (1, 0), (1, 1)),
    ((2, 0), (2, 1), (3, 0), (3, 1)),
    ((4, 0), (4, 1), (5, 0), (5, 1)),
    ((7, 0), (7, 1), (6, 0)),
    ((6, 1),),
)


def general_body(
    integrals,
    tile_mask,
    tile_owner,
    occupied_tiles,
    occupied_offsets,
    virtual_tiles,
    virtual_offsets,
):
    aux_local, basis_size, local_width = integrals.shape
    tile_width = basis_size // NT
    kcount = occupied_offsets.shape[0]
    local_tiles = local_width // tile_width
    group_index = lax.axis_index("grp")
    local_owner = lax.dynamic_slice_in_dim(tile_owner, group_index * local_tiles, local_tiles)
    matches = (local_owner[None, :, None] == jnp.arange(NT, dtype=jnp.int32)[None, None, :]).astype(
        jnp.int32
    )
    column_mask = jnp.sum(tile_mask[:, None, :] * matches, axis=2)
    blocked = integrals.reshape(aux_local, NT, tile_width, local_tiles, tile_width)
    masked = blocked * column_mask.astype(jnp.bfloat16)[None, :, None, :, None]
    masked = masked.reshape(aux_local, NT, tile_width, local_width)
    occupied_all, virtual_all = (
        lax.all_gather(occupied_tiles, ("grp", "blk"), axis=0, tiled=True),
        lax.all_gather(virtual_tiles, ("grp", "blk"), axis=0, tiled=True),
    )
    occupied_all = occupied_all.reshape(NT, kcount, tile_width, tile_width)
    virtual_all = virtual_all.reshape(NT, kcount, tile_width, tile_width)
    source_rows = (tile_owner[:, None] - occupied_offsets[None, :]) % NT
    partner_rows = (tile_owner[:, None] + virtual_offsets[None, :]) % NT
    virtual_pick = virtual_all[tile_owner]
    occupied_sum = jnp.zeros((aux_local, NT, tile_width, local_width), jnp.float32)
    virtual_sum = jnp.zeros((aux_local, local_width, NT, tile_width), jnp.float32)
    for slot in range(kcount):
        occupied_pick = occupied_all[source_rows[:, slot], slot]
        occupied_inputs = masked[:, source_rows[:, slot]]
        occupied_sum = occupied_sum + jnp.einsum(
            "tmn,ptml->ptnl", occupied_pick, occupied_inputs, preferred_element_type=jnp.float32
        )
        virtual_inputs = masked[:, partner_rows[:, slot]]
        virtual_sum = virtual_sum + jnp.einsum(
            "tnm,ptml->pltn",
            virtual_pick[:, slot],
            virtual_inputs,
            preferred_element_type=jnp.float32,
        )
    occupied_part = occupied_sum.astype(jnp.bfloat16)
    virtual_part = virtual_sum.astype(jnp.bfloat16).reshape(
        aux_local, local_tiles, tile_width, basis_size
    )
    occupied_moved = lax.all_to_all(occupied_part, "grp", split_axis=1, concat_axis=3, tiled=True)
    occupied_full, virtual_full = (
        lax.all_to_all(occupied_moved, "blk", split_axis=2, concat_axis=0, tiled=True),
        lax.all_to_all(virtual_part, "blk", split_axis=2, concat_axis=0, tiled=True),
    )
    left_side = occupied_full.reshape(occupied_full.shape[0], -1)
    right_side = virtual_full.reshape(virtual_full.shape[0], -1)
    partial_sum = jnp.einsum(
        "pe,qe->pq", left_side, right_side, preferred_element_type=jnp.float32
    ) * (1.0 / basis_size)
    total = lax.psum(partial_sum, ("grp", "blk"))
    return lax.dynamic_slice_in_dim(total, lax.axis_index("blk") * aux_local, aux_local, 0)


def place(refs, tile_row, column):
    owner_ref, mask_ref = refs
    return mask_ref[tile_row * NT + owner_ref[column]]


def masked_tile(values, kept):
    return values * jnp.full(values.shape, kept, jnp.int32).astype(values.dtype)


def picked_kernel(columns, planes_of, where_ref, owner_ref, mask_ref, *refs):
    inputs, out_ref = refs[:-1], refs[-1]
    tile = out_ref.shape[1]
    group = where_ref[0]
    row_plane = planes_of(pl.program_id(0)) ^ group
    for q in range(columns):
        tile_row = owner_ref[row_plane * columns + q]
        for c in range(columns):
            lanes = slice(c * tile, (c + 1) * tile)
            kept = place((owner_ref, mask_ref), tile_row, group * columns + c)
            out_ref[q, :, lanes] = masked_tile(inputs[q][0, 0, :, lanes], kept)


def triangle(columns):
    return [(q, c) for q in range(columns) for c in range(q + 1)]


def picked_square_kernel(columns, planes, where_ref, owner_ref, mask_ref, *refs):
    inputs, out_ref = refs[:-1], refs[-1]
    tile = out_ref.shape[1]
    first = where_ref[0] * columns
    wanted = [(0, q, c) for q, c in triangle(columns)]
    wanted += [(i, q, c) for i in range(1, len(planes)) for q in range(columns) for c in range(columns)]
    for at, (i, q, c) in enumerate(wanted):
        row = owner_ref[(where_ref[0] ^ planes[i]) * columns + q]
        kept = place((owner_ref, mask_ref), row, first + c)
        out_ref[at] = masked_tile(inputs[i * columns + q][0, 0, :, c * tile : (c + 1) * tile], kept)


def picked_square(scalars, integrals, away, planes=(0,)):
    aux_local, basis_size, width = integrals.shape
    tile = basis_size // NT
    columns = width // tile
    count = len(triangle(columns)) + (len(planes) - 1) * columns * columns

    def row_map(plane, q):
        def index(i, where, owner, mask):
            return (where[0] ^ away, owner[(where[0] ^ plane) * columns + q], 0, 0)

        return index

    return pl.pallas_call(
        functools.partial(picked_square_kernel, columns, planes),
        grid_spec=pltpu.PrefetchScalarGridSpec(
            num_scalar_prefetch=3,
            grid=(1,),
            in_specs=[
                pl.BlockSpec((1, 1, tile, width), row_map(plane, q))
                for plane in planes
                for q in range(columns)
            ],
            out_specs=pl.BlockSpec((count, tile, tile), lambda i, *_: (0, 0, 0)),
        ),
        out_shape=jax.ShapeDtypeStruct((count, tile, tile), jnp.bfloat16),
        compiler_params=pltpu.CompilerParams(vmem_limit_bytes=VMEM_BYTES),
        cost_estimate=pl.CostEstimate(flops=0, bytes_accessed=0, transcendentals=0),
        name="picked_square",
    )(*scalars, *([integrals.reshape(aux_local, NT, tile, width)] * (columns * len(planes))))


def picked_rows(scalars, integrals, away, row_planes):
    aux_local, basis_size, width = integrals.shape
    tile = basis_size // NT
    columns = width // tile

    def planes_of(i):
        return sum(jnp.where(i == at, plane, 0) for at, plane in enumerate(row_planes))

    def row_map(q):
        def index(i, where, owner, mask):
            plane = planes_of(i) ^ where[0]
            return (where[0] ^ away, owner[plane * columns + q], 0, 0)

        return index

    return pl.pallas_call(
        functools.partial(picked_kernel, columns, planes_of),
        grid_spec=pltpu.PrefetchScalarGridSpec(
            num_scalar_prefetch=3,
            grid=(len(row_planes),),
            in_specs=[pl.BlockSpec((1, 1, tile, width), row_map(q)) for q in range(columns)],
            out_specs=pl.BlockSpec((columns, tile, width), lambda i, *_: (i, 0, 0)),
        ),
        out_shape=jax.ShapeDtypeStruct((len(row_planes) * columns, tile, width), jnp.bfloat16),
        compiler_params=pltpu.CompilerParams(vmem_limit_bytes=VMEM_BYTES),
        cost_estimate=pl.CostEstimate(flops=0, bytes_accessed=0, transcendentals=0),
        name="picked_rows",
    )(*scalars, *([integrals.reshape(aux_local, NT, tile, width)] * columns))


def strips_of(columns):
    square = columns * columns
    return 2 * square, columns * 3 // 4 + (square - columns) // 2 + square // 2


def diagonal_strips(tiles, turned):
    rows, lanes = tiles[0].shape[-2] // 2, tiles[0].shape[-1] // 2
    shape = tiles[0].shape[:-2] + (rows, 2 * lanes)
    left = lax.broadcasted_iota(jnp.int32, shape, len(shape) - 1) < lanes
    kept, rest = [], []
    for c in range(0, len(tiles), 2):
        lower, upper = tiles[c][..., rows:, :], tiles[c + 1][..., :rows, :]
        if turned:
            lower = lower + jnp.where(left, tiles[c].T[rows:, :], 0)
            upper = upper + jnp.where(left, 0, tiles[c + 1].T[:rows, :])
        kept += [lower, upper]
        rest.append(jnp.where(left, tiles[c][..., :rows, :], tiles[c + 1][..., rows:, :]))
    halves = kept + rest
    return [
        jnp.concatenate(halves[at : at + 2], axis=-2) for at in range(0, len(halves), 2)
    ]


def pair_kernel(columns, where_ref, owner_ref, mask_ref, *refs):
    inputs, out_refs, (whole,) = refs[:columns], refs[columns:-1], refs[-1:]
    rows, tile = out_refs[0].shape[3:]
    first = where_ref[0] * columns
    step = pl.program_id(0)
    plane = where_ref[0] ^ pair_plane(step)
    cross, _ = strips_of(columns)
    within = cross + columns * 3 // 4
    sibling = within + (columns * columns - columns) // 2
    starts = [
        [(pl.multiple_of((part ^ where_ref[1]) * rows, rows), at) for part, at in some]
        for some in PARTS
    ]

    def masked(q, c):
        kept = place((owner_ref, mask_ref), owner_ref[plane * columns + q], first + c)
        return masked_tile(inputs[q][:, 0, :, c * tile : (c + 1) * tile], kept)

    def write(strip, strips):
        for at, values in enumerate(strips):
            whole[at] = values
        for out_ref, some in zip(out_refs, starts):
            count = out_ref.shape[1]
            for piece, (start, aux) in enumerate(some):
                for at in range(len(strips)):
                    out_ref[piece, :, strip + at] = whole[
                        at, aux * count : (aux + 1) * count, pl.ds(start, rows), :
                    ]

    @pl.when(step < 2)
    def _():
        for q in range(columns):
            write((step * columns + q) * columns, [masked(q, c) for c in range(columns)])

    @pl.when(step == 2)
    def _():
        write(cross, diagonal_strips([masked(c, c) for c in range(columns)], False))
        write(within, [masked(q, c) for q in range(columns) for c in range(q)])

    @pl.when((step == 3) & (where_ref[0] % 2 == 0))
    def _():
        write(sibling, [masked(q, c) for q in range(columns // 2) for c in range(columns)])

    @pl.when((step == 3) & (where_ref[0] % 2 == 1))
    def _():
        write(
            sibling, [masked(q, c) for q in range(columns) for c in range(columns // 2, columns)]
        )


def pair_plane(k):
    return jnp.where(k < 2, k + 2, k - 2)


def pair_tiles(scalars, integrals, parts):
    aux_local, basis_size, width = integrals.shape
    tile = basis_size // NT
    columns = width // tile
    rows = tile // parts
    shapes = [
        (len(some), aux_local // 2, sum(strips_of(columns)), rows, tile) for some in PARTS
    ]

    def row_map(q):
        def index(i, where, owner, mask):
            return (0, owner[(where[0] ^ pair_plane(i)) * columns + q], 0, 0)

        return index

    return pl.pallas_call(
        functools.partial(pair_kernel, columns),
        grid_spec=pltpu.PrefetchScalarGridSpec(
            num_scalar_prefetch=3,
            grid=(NT // columns,),
            in_specs=[
                pl.BlockSpec((aux_local, 1, tile, width), row_map(q)) for q in range(columns)
            ],
            out_specs=[pl.BlockSpec(shape, lambda i, *_: (0, 0, 0, 0, 0)) for shape in shapes],
            scratch_shapes=[
                pltpu.VMEM((columns * columns // 2, aux_local, tile, tile), jnp.bfloat16)
            ],
        ),
        out_shape=[jax.ShapeDtypeStruct(shape, jnp.bfloat16) for shape in shapes],
        compiler_params=pltpu.CompilerParams(vmem_limit_bytes=VMEM_BYTES),
        cost_estimate=pl.CostEstimate(flops=0, bytes_accessed=0, transcendentals=0),
        name="pair_tiles",
    )(*scalars, *([integrals.reshape(aux_local, NT, tile, width)] * columns))


def start_all(copies):
    for copy in copies:
        copy.start()


def wait_all(copies):
    for copy in copies:
        copy.wait()


def green_copies(green_refs, which, green, sems):
    copies = []
    for ref in green_refs:
        held = ref.shape[2]
        for plane in range(ref.shape[0]):
            at = len(copies)
            copies.append(
                pltpu.make_async_copy(
                    ref.at[plane, which], green.at[pl.ds(at * held, held)], sems.at[at]
                )
            )
    return copies


def column_planes(column_blocks, block_refs, tile, full):
    width = full.shape[1] // len(column_blocks)
    columns = width // tile
    for at, blocks in enumerate(column_blocks):
        for plane, (ref, first, turned) in enumerate(blocks):
            if first is None:
                for i, (q, c) in enumerate(triangle(columns)):
                    row, column = plane * width + q * tile, at * width + c * tile
                    values = block_refs[ref][i]
                    full[row : row + tile, column : column + tile] = values
                    if q != c:
                        row, column = plane * width + c * tile, at * width + q * tile
                        full[row : row + tile, column : column + tile] = values.T
                continue
            if block_refs[ref].shape[2] == tile:
                count = len(triangle(columns)) + (first - 1) * columns * columns
                for i in range(columns * columns):
                    q, c = i // columns, i % columns
                    if turned:
                        q, c = c, q
                    row, column = plane * width + q * tile, at * width + c * tile
                    values = block_refs[ref][count + i]
                    full[row : row + tile, column : column + tile] = values.T if turned else values
                continue
            values = block_refs[ref][first * columns : (first + 1) * columns]
            values = values.reshape(width, width)
            full[plane * width : (plane + 1) * width, at * width : (at + 1) * width] = (
                values.T if turned else values
            )


def occupied_rows(kcount, count, width, slot_ref, tile_ref, green, full, half, first, start, stop):
    tile = green.shape[1]
    columns = width // tile

    @pl.loop(start, stop, unroll=UNROLL)
    def _(r):
        left = jnp.concatenate([green[tile_ref[r * kcount + k]] for k in range(kcount)], axis=1)
        starts = [pl.multiple_of(slot_ref[r * kcount + k] * tile, tile) for k in range(kcount)]
        rows = pl.ds(pl.multiple_of(r * tile, tile), tile)
        for at in range(count):
            right = jnp.concatenate(
                [full[pl.ds(start, tile), at * width : (at + 1) * width] for start in starts],
                axis=0,
            )
            values = jnp.dot(left, right, preferred_element_type=jnp.float32).astype(jnp.bfloat16)
            for c in range(columns):
                half[first + at * columns + c, rows, :] = values[:, c * tile : (c + 1) * tile]


def half_products(kcount, other, slot_ref, tile_ref, green, half, product):
    tile = green.shape[1]
    count = NT // 2

    def column(t, rows):
        right = jnp.concatenate([green[tile_ref[t * kcount + k]] for k in range(kcount)], axis=0)
        slots = [slot_ref[t * kcount + k] for k in range(kcount)]
        for first in range(0, count, 4):
            start = (rows + first) * tile
            left = jnp.concatenate(
                [half[slot, start : start + 4 * tile, :] for slot in slots], axis=1
            )
            values = jnp.dot(left, right, preferred_element_type=jnp.float32)
            product[t, first : first + 4] = values.reshape(4, tile, tile)

    pl.loop(0, count, unroll=UNROLL)(lambda t: column(t, count if other else 0))
    pl.loop(count, NT, unroll=UNROLL)(lambda t: column(t, 0 if other else count))


def write_strip(out_ref, device, strip, values):
    rows = out_ref.shape[2]
    values = values.astype(jnp.bfloat16)
    for part in range(values.shape[0] // rows):
        out_ref[device + part, strip] = values[part * rows : (part + 1) * rows]


def cross_strips(columns, group, product, out_ref):
    count = NT // 2
    parts = out_ref.shape[0] // 2

    @pl.loop(0, 2)
    def _(plane):
        away = plane ^ lax.rem(group, 2)

        @pl.loop(0, 2)
        def _(k):
            first = (k ^ away) * columns
            for q in range(columns):
                for c in range(columns):
                    s = away * columns + c
                    values = product[s, first + q] + product[count + first + q, s].T
                    write_strip(out_ref, plane * parts, (k * columns + q) * columns + c, values)


def within_strips(columns, group, product, out_ref):
    planes = NT // columns
    parts = out_ref.shape[0] // planes

    for plane in range(planes):
        away = plane ^ group
        own, near = lax.rem(away, 2) * columns, (1 - lax.rem(away, 2)) * columns
        first, sibling = away * columns, (away ^ 1) * columns
        tiles = [product[first + c, own + c] for c in range(columns)]
        strips = diagonal_strips(tiles, True)
        for q in range(columns):
            for c in range(q):
                strips.append(product[first + c, own + q] + product[first + q, own + c].T)
        for at in range(columns * columns // 2):
            if plane % 2:
                q, c = at // (columns // 2), columns // 2 + at % (columns // 2)
            else:
                q, c = at // columns, at % columns
            strips.append(product[first + c, near + q] + product[sibling + q, own + c].T)
        for strip, values in enumerate(strips):
            write_strip(out_ref, plane * parts, strip, values)


def first_kernel(
    kcount, columns, column_blocks, parts, group_ref, slot_ref, tile_ref, half_slot_ref,
    virtual_tile_ref, *refs
):
    green_refs, refs = refs[:parts], refs[parts:]
    block_refs, refs = refs[:-9], refs[-9:]
    out_ref, half_ref, green, virtual, full, half, product, sems, others = refs
    width = full.shape[1] // len(column_blocks)
    copies = green_copies(green_refs, 0, green, sems)
    start_all(copies)
    column_planes(column_blocks, block_refs, green.shape[1], full)
    wait_all(copies)
    later = green_copies(green_refs, 1, virtual, others)
    start_all(later)
    occupied_rows(
        kcount, len(column_blocks), width, slot_ref, tile_ref, green, full, half, 0, 0, NT
    )
    kept = pltpu.make_async_copy(half, half_ref, others.at[others.shape[0] - 1])
    kept.start()
    wait_all(later)
    half_products(kcount, False, half_slot_ref, virtual_tile_ref, virtual, half, product)
    within_strips(columns, group_ref[0], product, out_ref)
    kept.wait()


def rest_kernel(
    kcount, columns, parts, group_ref, half_slot_ref, virtual_tile_ref, *refs
):
    green_refs, refs = refs[:parts], refs[parts:]
    half_ref, out_ref, virtual, half, product, others = refs
    copies = green_copies(green_refs, 1, virtual, others)
    copies.append(pltpu.make_async_copy(half_ref, half, others.at[others.shape[0] - 1]))
    start_all(copies)
    wait_all(copies)
    half_products(kcount, True, half_slot_ref, virtual_tile_ref, virtual, half, product)
    cross_strips(columns, group_ref[0], product, out_ref)


def kernel_call(
    kernel, tables, anywhere, blocks, out_shape, out_spaces, scratch_shapes, name, flops=0
):
    return pl.pallas_call(
        kernel,
        in_specs=[pl.BlockSpec(memory_space=pltpu.SMEM)] * len(tables)
        + [pl.BlockSpec(memory_space=pl.ANY)] * len(anywhere)
        + [pl.BlockSpec(memory_space=pltpu.VMEM)] * len(blocks),
        out_specs=[pl.BlockSpec(memory_space=space) for space in out_spaces],
        out_shape=out_shape,
        scratch_shapes=scratch_shapes,
        compiler_params=pltpu.CompilerParams(vmem_limit_bytes=VMEM_BYTES),
        cost_estimate=pl.CostEstimate(flops=flops, bytes_accessed=flops // 512, transcendentals=0),
        name=name,
    )(*tables, *anywhere, *blocks)


def arranged_kernel(first, parts, where_ref, *refs):
    right_refs, (out_ref, right, sems) = refs[:parts], refs[parts:]
    others, count, rows, tile = right.shape
    copies = []
    at = 0
    for i, ref in enumerate(right_refs):
        place_at = (at // 4 ^ where_ref[1]) * 4 + at % 4
        copies.append(
            pltpu.make_async_copy(
                ref.at[:, pl.ds(first, count)],
                right.at[pl.ds(place_at, ref.shape[0])],
                sems.at[i],
            )
        )
        at += ref.shape[0]
    start_all(copies)
    wait_all(copies)
    for i in range(count):
        out_ref[:, i * tile : (i + 1) * tile] = right[:, i].reshape(others * rows, tile)


def arranged(where, rights, first, count):
    parts = len(rights)
    rows, tile = rights[0].shape[2:]
    others = sum(each.shape[0] for each in rights)
    return pl.pallas_call(
        functools.partial(arranged_kernel, first, parts),
        in_specs=[pl.BlockSpec(memory_space=pltpu.SMEM)]
        + [pl.BlockSpec(memory_space=pl.ANY)] * parts,
        out_specs=pl.BlockSpec(memory_space=pltpu.VMEM),
        out_shape=jax.ShapeDtypeStruct((others * rows, count * tile), jnp.bfloat16),
        scratch_shapes=[
            pltpu.VMEM((others, count, rows, tile), jnp.bfloat16),
            pltpu.SemaphoreType.DMA((parts,)),
        ],
        compiler_params=pltpu.CompilerParams(vmem_limit_bytes=PAIRED_BYTES),
        name="arranged",
    )(where, *rights)


def paired_kernel(columns, where_ref, left_ref, right_ref, *refs):
    base_refs, (out_ref, sums) = refs[:-2], refs[-2:]
    sources, count, rows, tile = left_ref.shape
    others = sums.shape[0]
    values = lax.dot_general(
        jnp.concatenate([left_ref[:, i].reshape(sources * rows, tile) for i in range(count)], axis=1),
        right_ref[...],
        (((1,), (1,)), ((), ())),
        preferred_element_type=jnp.float32,
    )
    down = lax.broadcasted_iota(jnp.int32, values.shape, 0)
    along = lax.broadcasted_iota(jnp.int32, values.shape, 1)
    values = jnp.where((down ^ along) % rows == 0, values, 0.0)
    values = jnp.sum(values.reshape(sources, rows, others * rows), axis=1)
    values = jnp.sum(values.T.reshape(others, rows, sources), axis=1).T
    if not base_refs:
        out_ref[...] = values
        return
    devices = out_ref.shape[0]
    each = devices // columns
    start = pl.multiple_of(where_ref[0] // 2 * sources, sources)
    out_ref[...] = jnp.zeros_like(out_ref)
    sums[...] = base_refs[0][...]
    sums[pl.ds(start, sources), :] += values
    for blk in range(each):
        values = sums[pl.ds(blk, columns, stride=each), :] * (1.0 / (NT * tile))
        for plane in range(columns):
            out_ref[plane * each + blk, :columns, :others] = values


def paired(where, left, rights, first, base=None):
    sources, count, rows, tile = left.shape
    others = sum(each.shape[0] for each in rights)
    vmem = pl.BlockSpec(memory_space=pltpu.VMEM)
    base = () if base is None else (base,)
    shape = (base[0].shape[0], 8, 128) if base else (sources, others)
    return pl.pallas_call(
        functools.partial(paired_kernel, 4),
        in_specs=[
            pl.BlockSpec(memory_space=pltpu.SMEM),
            vmem,
            vmem,
        ]
        + [vmem] * len(base),
        out_specs=vmem,
        out_shape=jax.ShapeDtypeStruct(shape, jnp.float32),
        scratch_shapes=[
            pltpu.VMEM((others, others), jnp.float32),
        ],
        compiler_params=pltpu.CompilerParams(vmem_limit_bytes=PAIRED_BYTES),
        name="paired",
    )(where, left, arranged(where, rights, first, count), *base)


def folded_body(
    integrals,
    tile_mask,
    tile_owner,
    occupied_tiles,
    occupied_offsets,
    virtual_tiles,
    virtual_offsets,
):
    aux_local, basis_size, width = integrals.shape
    tile = basis_size // NT
    columns = width // tile
    planes, parts = lax.axis_size("grp"), lax.axis_size("blk")
    kcount = occupied_offsets.shape[0]
    group = lax.axis_index("grp")

    part = lax.axis_index("blk")
    scalars = (
        jnp.stack([group, part]).astype(jnp.int32),
        tile_owner,
        tile_mask.reshape(-1),
    )

    def swap(values, axis, size, distance):
        return lax.ppermute(values, axis, [(at, at ^ distance) for at in range(size)])

    greens = jnp.stack(
        [
            jnp.swapaxes(occupied_tiles.reshape(-1, tile, tile), 1, 2),
            virtual_tiles.reshape(-1, tile, tile),
        ]
    )
    held = greens.shape[1]
    greens = jnp.stack([greens] + [swap(greens, "grp", planes, j) for j in range(1, planes)])
    pairs = list(pair_tiles(scalars, integrals, parts))
    pairs[3] = swap(pairs[3], "blk", parts, 6)
    near_off = picked_rows(scalars, integrals, 1, (3, 2))
    across = picked_square(scalars, integrals, 2, (0, 1))

    slot = jnp.arange(NT, dtype=jnp.int32)
    ordered = jnp.zeros((NT,), jnp.int32).at[tile_owner].set(slot)
    ordered = (ordered // columns ^ group) * columns + ordered % columns
    nearby = (slot // columns ^ group) * columns + slot % columns

    def table(targets, offsets):
        natural = (targets[:, None] - offsets[None, :]) % NT
        flat = natural * kcount + jnp.arange(kcount, dtype=jnp.int32)[None, :]
        device = flat // held
        plane, other = device // parts ^ group, device % parts ^ part
        at = ((other * planes + plane) * held) + flat % held
        return ordered[natural].reshape(-1), at.reshape(-1)

    occupied_table = table(tile_owner[nearby], occupied_offsets)
    virtual_table = table(tile_owner[nearby], virtual_offsets)

    greens, near_off, across, scalars = lax.optimization_barrier(
        (greens, near_off, across, scalars)
    )
    greens = [greens] + [swap(greens, "blk", parts, m) for m in (2, 4)]
    near_off = swap(near_off, "grp", planes, 1)
    across = swap(across, "grp", planes, 2)
    near = picked_square(scalars, integrals, 1)
    far = picked_square(scalars, integrals, 3)

    greens, near_off, across, near, far, pairs, scalars = lax.optimization_barrier(
        (greens, near_off, across, near, far, pairs, scalars)
    )
    greens = [
        greens[0],
        greens[1],
        swap(greens[1], "blk", parts, 1),
        greens[2],
        swap(greens[1][: planes // 2], "blk", parts, 4),
        swap(greens[2][planes // 2 :], "blk", parts, 2),
    ]
    near = swap(near, "grp", planes, 1)
    far = swap(far, "grp", planes, 3)
    own = picked_rows(scalars, integrals, 0, (0, 1, 2, 3))

    greens, near, far, own, pairs, occupied_table, virtual_table = lax.optimization_barrier(
        (greens, near, far, own, pairs, occupied_table, virtual_table)
    )
    greens = [
        greens[0],
        swap(greens[0], "blk", parts, 1),
        *greens[1:4],
        swap(greens[3], "blk", parts, 1),
        *greens[4:],
        swap(greens[4], "blk", parts, 1),
        swap(greens[5], "blk", parts, 1),
    ]
    for m in (1, 2):
        pairs[m] = swap(pairs[m], "blk", parts, 2 * m)

    where = scalars[0]

    def vmem(*shape, dtype=jnp.bfloat16):
        return pltpu.VMEM(shape, dtype)

    devices = planes * parts
    green = vmem(devices * held, tile, tile)

    cross, within = strips_of(columns)

    def strips(count, strips):
        return jax.ShapeDtypeStruct((count, strips, tile // parts, tile), jnp.bfloat16)

    product = vmem(NT, NT // 2, tile, tile, dtype=jnp.float32)

    column_blocks = (
        ((0, 0, False), (0, 1, False), (0, 2, False), (0, 3, False)),
        ((0, 1, True), (1, None, False), (2, 0, False), (2, 1, False)),
        ((0, 2, True), (2, 0, True), (3, None, False), (3, 1, False)),
        ((0, 3, True), (2, 1, True), (3, 1, True), (4, None, False)),
    )
    half = vmem(NT, basis_size, tile)
    sent, halves = kernel_call(
        functools.partial(first_kernel, kcount, columns, column_blocks, len(greens)),
        (where,) + occupied_table + virtual_table,
        greens,
        (own, near, near_off, across, far),
        [strips(devices, within), jax.ShapeDtypeStruct((NT, basis_size, tile), jnp.bfloat16)],
        [pltpu.VMEM, pl.ANY],
        [
            green,
            green,
            vmem(basis_size, basis_size),
            half,
            product,
            pltpu.SemaphoreType.DMA((devices,)),
            pltpu.SemaphoreType.DMA((devices + 1,)),
        ],
        "half_and_pairs",
    )
    sent, halves, pairs = lax.optimization_barrier((sent, halves, pairs))
    pairs[4] = swap(pairs[4], "blk", parts, 6)
    pairs[3:] = [pairs[3][2:], pairs[4], swap(pairs[3][:2], "blk", parts, 1)]
    pairs = [
        each
        for mine in pairs[:3]
        for each in (mine[:2], swap(mine[2:], "blk", parts, 1))
    ] + pairs[3:]
    (rest,) = kernel_call(
        functools.partial(rest_kernel, kcount, columns, len(greens)),
        (where,) + virtual_table,
        [*greens, halves],
        (),
        [strips(2 * parts, cross)],
        [pltpu.VMEM],
        [
            green,
            half,
            product,
            pltpu.SemaphoreType.DMA((devices + 1,)),
        ],
        "other_pairs",
        flops=2 * 8 * basis_size * kcount * tile * tile * 2,
    )

    def everyone(values, groups=None):
        return lax.all_to_all(
            values, ("grp", "blk"), split_axis=0, concat_axis=0, tiled=True,
            axis_index_groups=groups,
        )

    sent = everyone(sent)
    sent, rest, pairs = lax.optimization_barrier((sent, rest, pairs))
    rest = everyone(rest, [list(range(2 * parts)), list(range(2 * parts, devices))])
    pairs = [each.reshape((-1,) + each.shape[2:]) for each in pairs]

    total = paired(where, sent, pairs, cross)
    total = jnp.sum(everyone(paired(where, rest, pairs, 0, total)), axis=0)
    return total[:aux_local, : parts * aux_local]


def solution(mesh):
    planes, parts = mesh.shape["grp"], mesh.shape["blk"]

    def body(*args):
        aux_local, basis_size, width = args[0].shape
        tile = basis_size // NT
        fits = aux_local == planes == 4 and parts == 8 and width % tile == 0 and tile % (16 * parts) == 0 and width == 4 * tile
        return (folded_body if fits else general_body)(*args)

    in_specs = (
        P("blk", None, "grp"),
        P(),
        P(),
        P(("grp", "blk"), None),
        P(),
        P(("grp", "blk"), None),
        P(),
    )
    out_specs = P("blk", None)
    return jax.shard_map(body, mesh=mesh, in_specs=in_specs, out_specs=out_specs, check_vma=False)
```
